256 devices in a mesh: row: 16 (over z_hi, x), col: 16 (over z_lo, y, core).
Axes of the slice: x: 4, y: 4, z: 8 (z_hi: 4, z_lo: 2; z = z_hi * 2 + z_lo), core: 2. Of those that a mesh axis runs over, the one named last changes fastest.
Arguments:
- embeddings: float32 [32768, 512], P(('row', 'col')), may hold values from -6 to 6
- margin: int32 [32768], P(('row', 'col')), may hold values from 0 to 99
- group: int32 [32768], P(('row', 'col')), may hold values from 0 to 7
Outputs:
- updated: float32 [32768, 512], P(('row', 'col'))
The draws below stay inside these ranges and needn't reach their ends.
All inputs are finite; a program needn't handle non-finite values.
Results may differ from the reference program's by a relative error of at most 0.005.
Values may be sent and summed in bfloat16 or wider, within the bound.
No kernel may reach another device: no remote copies, remote signals or barrier semaphores. Data moves between devices by JAX's collectives and lax.ppermute only.
A program may use at most 64 MiB of HBM per device.

```python
import math
import jax
import jax.numpy as jnp
from jax import lax

D = 512
CPD = 128
GROUPS = 8
CLASSES = 32768


def with_ends(values, stream_key, least, largest):
    longest = values.shape.index(max(values.shape))
    spots = []
    for shift in (0, 1):
        where = [jax.random.randint(jax.random.fold_in(stream_key, axis), (), 0, length) for axis, length in enumerate(values.shape)]
        where[longest] = (where[longest] + shift) % values.shape[longest]
        spots.append(tuple(where))
    return values.at[spots[0]].set(least).at[spots[1]].set(largest)


def block_scale(rng, shape, cuts, least, top_value):
    level, own = 1.0, jax.random.fold_in(rng, 6)
    for position, blocks in cuts:
        steps = jnp.exp(jax.random.uniform(jax.random.fold_in(own, position), (blocks,), jnp.float32, least / len(cuts), top_value / len(cuts)))
        level = level * jnp.repeat(steps, shape[position] // blocks).reshape([-1 if axis == position else 1 for axis in range(len(shape))])
    return level


def gaussian(key, extent, deviation, reach, shards=(), dtype=jnp.bfloat16):
    result = jax.random.normal(key, extent, jnp.float32) * deviation
    if len(shards) > 0:
        result = block_scale(key, extent, shards, -0.22, 0.18) * result
    return jnp.clip(result, min=-reach, max=reach).astype(dtype)


def setup_inputs(seed: int = 0) -> dict:
    key_list = jax.random.split(jax.random.key(seed), 4)
    return {
        "embeddings": gaussian(key_list[0], (CLASSES, D), 1.0, 6.0, ((0, 256),), jnp.float32),
        "margin": with_ends(jax.random.randint(key_list[1], (CLASSES,), 0, 100), jax.random.fold_in(key_list[1], 1), 0, 99).astype(jnp.int32),
        "group": with_ends(jax.random.randint(key_list[2], (CLASSES,), 0, GROUPS), jax.random.fold_in(key_list[2], 1), 0, GROUPS - 1).astype(jnp.int32),
    }


def reference(embeddings, margin, group):
    lengths = jnp.sqrt(lax.optimization_barrier(jnp.sum(embeddings * embeddings, axis=1)) + 1e-06)
    unit_rows = embeddings / lengths[:, None]
    unit_half = unit_rows.astype(jnp.bfloat16)
    unit_trans = unit_half.T
    blocks = CLASSES // CPD

    def tile_rows(pieces):
        piece_units, piece_margin, piece_group = pieces
        cosine = jnp.dot(piece_units, unit_trans, preferred_element_type=jnp.float32)
        pair_margin = (piece_margin[:, None] + margin[None, :]).astype(jnp.float32) * 0.0005
        slopes = jnp.where(piece_group[:, None] != group[None, :], 2.0 * jax.nn.relu(cosine - pair_margin), 0.0).astype(jnp.bfloat16)
        return 2.0 * jnp.dot(slopes, unit_half, preferred_element_type=jnp.float32)
    grad_units = lax.map(tile_rows, (unit_half.reshape(blocks, CPD, D), margin.reshape(blocks, CPD), group.reshape(blocks, CPD)))
    grad_units = grad_units.reshape(CLASSES, D)
    radial = lax.optimization_barrier(jnp.sum(unit_rows * grad_units, axis=1, keepdims=True))
    grad_rows = (grad_units - unit_rows * radial) / lengths[:, None]
    step_rate = D * math.sqrt(D) / (3.0 * math.sqrt(CLASSES))
    return embeddings - step_rate * grad_rows
```

```python
import functools
import itertools
import math

import jax
import jax.numpy as jnp
from jax import lax
from jax.experimental import pallas as pl
from jax.experimental.pallas import tpu as pltpu
from jax.sharding import PartitionSpec as P

BF = jnp.bfloat16
F32 = jnp.float32
D = 512
CPD = 128
HALF = CPD // 2
META = 16
LANES = 128
CHUNKS = D // LANES
ROWS_R = CHUNKS * CPD + META
ROWS_C = CHUNKS * HALF + META
AXES = ("row", "col")
VMEM = pl.BlockSpec(memory_space=pltpu.VMEM)
ANY = pl.BlockSpec(memory_space=pl.ANY)


def _flat(x, y, z, core):
    return ((((z // 2) * 4 + x) * 2 + z % 2) * 4 + y) * 2 + core


LINKS = {
    "xa": lambda x, y, z: (x ^ 1, y, z),
    "xb": lambda x, y, z: (3 - x, y, z),
    "ya": lambda x, y, z: (x, y ^ 1, z),
    "yb": lambda x, y, z: (x, 3 - y, z),
    "za": lambda x, y, z: (x, y, z ^ 1),
    "zb": lambda x, y, z: (x, y, (z - 1) % 8 if z % 2 == 0 else (z + 1) % 8),
}
RING = ("xa", "ya", "xb", "yb")


def swap(block, link0, link1):
    pairs = []
    for x, y, z, core in itertools.product(range(4), range(4), range(8), range(2)):
        pairs.append((_flat(x, y, z, core), _flat(*LINKS[(link0, link1)[core]](x, y, z), core)))
    return lax.ppermute(block, AXES, pairs)


def swap_cores(block):
    return lax.ppermute(block, AXES, [(i, i ^ 1) for i in range(256)])


def pack_kernel(emb, margin, group, whole, first, second):
    e = emb[...]
    unit = (e / jnp.sqrt(jnp.sum(e * e, axis=1, keepdims=True) + 1e-06)).astype(BF)
    row = lax.broadcasted_iota(jnp.int32, (META, LANES), 0)
    meta = jnp.where(row == 0, margin[...], jnp.where(row == 1, group[...], 0)).astype(F32).astype(BF)
    for f in range(CHUNKS):
        part = unit[:, f * LANES : (f + 1) * LANES]
        whole[f * CPD : (f + 1) * CPD, :] = part
        first[f * HALF : (f + 1) * HALF, :] = part[:HALF]
        second[f * HALF : (f + 1) * HALF, :] = part[HALF:]
    whole[CHUNKS * CPD :, :] = meta
    first[CHUNKS * HALF :, :] = meta
    second[CHUNKS * HALF :, :] = meta


def pack(embeddings, margin, group):
    shapes = [jax.ShapeDtypeStruct((r, LANES), BF) for r in (ROWS_R, ROWS_C, ROWS_C)]
    return pl.pallas_call(
        pack_kernel,
        out_shape=shapes,
        in_specs=[VMEM] * 3,
        out_specs=[VMEM] * 3,
        name="pack",
    )(embeddings, margin.reshape(1, CPD), group.reshape(1, CPD))


TILE = 1024


def pair_kernel(n_r, n_c, *refs):
    r_in, c_in, rest = refs[:n_r], refs[n_r : n_r + n_c], refs[n_r + n_c :]
    outs = rest[:n_r]
    rbuf, rmeta, cbuf, cmeta, rm, rg, acc, r_sem, c_sem = rest[n_r:]
    tiles = n_c // 2
    r_copies, c_copies = [], []
    at = 0
    for i, ref in enumerate(r_in):
        n = ref.shape[0]
        own = [
            pltpu.make_async_copy(
                ref.at[:, f * CPD : (f + 1) * CPD, :],
                rbuf.at[at : at + n, :, f * LANES : (f + 1) * LANES],
                r_sem.at[i, f],
            )
            for f in range(CHUNKS)
        ]
        own.append(pltpu.make_async_copy(ref.at[:, CHUNKS * CPD :, :], rmeta.at[at : at + n], r_sem.at[i, CHUNKS]))
        r_copies += own
        at += n

    def c_copy(ref, t, h):
        own = [
            pltpu.make_async_copy(
                ref.at[:, f * HALF : (f + 1) * HALF, :],
                cbuf.at[pl.ds(t * 8, 8), h * HALF : (h + 1) * HALF, f * LANES : (f + 1) * LANES],
                c_sem.at[t, h, f],
            )
            for f in range(CHUNKS)
        ]
        own.append(
            pltpu.make_async_copy(ref.at[:, CHUNKS * HALF :, :], cmeta.at[h, pl.ds(t * 8, 8)], c_sem.at[t, h, CHUNKS])
        )
        return own

    for c in r_copies:
        c.start()
    for t in range(tiles):
        for h in range(2):
            for c in c_copy(c_in[2 * t + h], t, h):
                c.start()
    for c in r_copies:
        c.wait()
    for k in range(at):
        m = rmeta[k].astype(F32)
        rm[k * CPD : (k + 1) * CPD, :] = jnp.broadcast_to(m[0:1] * 0.0005, (CPD, CPD)).T
        rg[k * CPD : (k + 1) * CPD, :] = jnp.broadcast_to(m[1:2], (CPD, CPD)).T
    acc[...] = jnp.zeros_like(acc)
    lane = lax.broadcasted_iota(jnp.int32, (1, LANES), 1)

    def body(t, carry):
        for h in range(2):
            for c in c_copy(c_in[h], t, h):
                c.wait()
        ct = cbuf[pl.ds(t * 8, 8)].reshape(TILE, D)
        margins, groups = [], []
        for k in range(8):
            m0 = cmeta[0, t * 8 + k].astype(F32)
            m1 = cmeta[1, t * 8 + k].astype(F32)
            margins.append(jnp.where(lane < HALF, m0[0:1], m1[0:1]) * 0.0005)
            groups.append(jnp.where(lane < HALF, m0[1:2], m1[1:2]))
        for r0 in range(0, at * CPD, 256):
            rt = rbuf[r0 // CPD : r0 // CPD + 2].reshape(256, D)
            cos = lax.dot_general(rt, ct, (((1,), (1,)), ((), ())), preferred_element_type=F32)
            parts = []
            for k in range(8):
                over = jnp.maximum(cos[:, k * LANES : (k + 1) * LANES] - rm[r0 : r0 + 256, :] - margins[k], 0.0)
                parts.append(jnp.where(rg[r0 : r0 + 256, :] != groups[k], over, 0.0).astype(BF))
            s = jnp.concatenate(parts, axis=1)
            acc[r0 : r0 + 256, :] += jnp.dot(s, ct, preferred_element_type=F32)
        return carry

    lax.fori_loop(0, tiles, body, 0)
    o = 0
    for out in outs:
        n = out.shape[0]
        out[...] = acc[o : o + n, :].astype(out.dtype)
        o += n


def pair(r_in, c_in, out_dtype):
    blocks = sum(a.shape[0] for a in r_in)
    rows, n_c = blocks * CPD, len(c_in)
    tiles = n_c // 2
    return pl.pallas_call(
        functools.partial(pair_kernel, len(r_in), n_c),
        out_shape=[jax.ShapeDtypeStruct((a.shape[0] * CPD, D), out_dtype) for a in r_in],
        in_specs=[ANY] * (len(r_in) + n_c),
        out_specs=[VMEM] * len(r_in),
        scratch_shapes=[
            pltpu.VMEM((blocks, CPD, D), BF),
            pltpu.VMEM((blocks, META, LANES), BF),
            pltpu.VMEM((tiles * 8, CPD, D), BF),
            pltpu.VMEM((2, tiles * 8, META, LANES), BF),
            pltpu.VMEM((rows, CPD), F32),
            pltpu.VMEM((rows, CPD), F32),
            pltpu.VMEM((rows, D), F32),
            pltpu.SemaphoreType.DMA((len(r_in), CHUNKS + 1)),
            pltpu.SemaphoreType.DMA((tiles, 2, CHUNKS + 1)),
        ],
        compiler_params=pltpu.CompilerParams(vmem_limit_bytes=40 << 20),
        cost_estimate=pl.CostEstimate(
            flops=4 * rows * tiles * TILE * D, bytes_accessed=(tiles * TILE + rows) * D * 2, transcendentals=0
        ),
        name="pair",
    )(*r_in, *c_in)


def final_kernel(rate, emb, own, arrived, out):
    e = emb[...]
    lengths = jnp.sqrt(jnp.sum(e * e, axis=1, keepdims=True) + 1e-06)
    unit = e / lengths
    grad = 4.0 * (own[...] + arrived[...].astype(F32))
    radial = jnp.sum(unit * grad, axis=1, keepdims=True)
    out[...] = e - rate * ((grad - unit * radial) / lengths)


def per_device(embeddings, margin, group):
    classes = embeddings.shape[0] * lax.axis_size("row") * lax.axis_size("col")
    whole, first, second = pack(embeddings, margin, group)

    def cat(a, b):
        return jnp.concatenate([a, b], axis=0)

    z1 = cat(whole, swap(whole, "za", "zb"))
    z2 = swap(z1, "zb", "za")
    z3 = swap(z2, "za", "zb")
    z4 = swap(z3, "zb", "za")
    held = []
    for start, block in ((0, first), (2, second)):
        for s in range(3):
            block = cat(block, swap(block, RING[(start + s) % 4], RING[(start + s + 1) % 4]))
        held.append((block, swap(block, RING[(start + 3) % 4], RING[start])))
    (a0, a1), (b0, b1) = held
    c_in = [a0, b0, swap_cores(a0), swap_cores(b0), a1, b1, swap_cores(a1), swap_cores(b1)]
    c_in = [a.reshape(-1, ROWS_C, LANES) for a in c_in]
    z1, z2, z3, z4 = (a.reshape(-1, ROWS_R, LANES) for a in (z1, z2, z3, z4))

    (p4,) = pair([z4], c_in, BF)
    q = swap(p4, "zb", "za")
    p1, p2, p3 = pair([z1, z2, z3], c_in, F32)
    q = swap((p3 + q).astype(BF), "za", "zb")
    q = swap((p2 + q).astype(BF), "zb", "za")
    own = p1 + q
    q = swap(own[CPD:].astype(BF), "za", "zb")

    rate = D * math.sqrt(D) / (3.0 * math.sqrt(classes))
    return pl.pallas_call(
        functools.partial(final_kernel, rate),
        out_shape=jax.ShapeDtypeStruct((CPD, D), F32),
        in_specs=[VMEM] * 3,
        out_specs=VMEM,
        name="final",
    )(embeddings, own[:CPD], q)


def solution(mesh):
    in_specs = (P(("row", "col"), None), P(("row", "col")), P(("row", "col")))
    out_specs = P(("row", "col"), None)
    return jax.shard_map(per_device, mesh=mesh, in_specs=in_specs, out_specs=out_specs, check_vma=False)
```

```python
import functools
import itertools
import math

import jax
import jax.numpy as jnp
from jax import lax
from jax.experimental import pallas as pl
from jax.experimental.pallas import tpu as pltpu
from jax.sharding import PartitionSpec as P

BF = jnp.bfloat16
F32 = jnp.float32
D = 512
CPD = 128
HALF = CPD // 2
META = 16
LANES = 128
CHUNKS = D // LANES
ROWS_R = CHUNKS * CPD + META
ROWS_C = CHUNKS * HALF + META
SMALL = 6 << 20
AXES = ("row", "col")
VMEM = pl.BlockSpec(memory_space=pltpu.VMEM)
ANY = pl.BlockSpec(memory_space=pl.ANY)


def _flat(x, y, z, core):
    return ((((z // 2) * 4 + x) * 2 + z % 2) * 4 + y) * 2 + core


LINKS = {
    "xa": lambda x, y, z: (x ^ 1, y, z),
    "xb": lambda x, y, z: (3 - x, y, z),
    "ya": lambda x, y, z: (x, y ^ 1, z),
    "yb": lambda x, y, z: (x, 3 - y, z),
    "za": lambda x, y, z: (x, y, z ^ 1),
    "zb": lambda x, y, z: (x, y, (z - 1) % 8 if z % 2 == 0 else (z + 1) % 8),
}
RING = ("xa", "ya", "xb", "yb")


def swap(block, link0, link1):
    pairs = []
    for x, y, z, core in itertools.product(range(4), range(4), range(8), range(2)):
        pairs.append((_flat(x, y, z, core), _flat(*LINKS[(link0, link1)[core]](x, y, z), core)))
    return lax.ppermute(block, AXES, pairs)


def swap_cores(block):
    return lax.ppermute(block, AXES, [(i, i ^ 1) for i in range(256)])


def pack_kernel(emb, margin, group, whole, first, second):
    e = emb[...]
    unit = (e / jnp.sqrt(jnp.sum(e * e, axis=1, keepdims=True) + 1e-06)).astype(BF)
    row = lax.broadcasted_iota(jnp.int32, (META, LANES), 0)
    meta = jnp.where(row == 0, margin[...], jnp.where(row == 1, group[...], 0)).astype(F32).astype(BF)
    for f in range(CHUNKS):
        part = unit[:, f * LANES : (f + 1) * LANES]
        whole[f * CPD : (f + 1) * CPD, :] = part
        first[f * HALF : (f + 1) * HALF, :] = part[:HALF]
        second[f * HALF : (f + 1) * HALF, :] = part[HALF:]
    whole[CHUNKS * CPD :, :] = meta
    first[CHUNKS * HALF :, :] = meta
    second[CHUNKS * HALF :, :] = meta


def pack(embeddings, margin, group):
    shapes = [jax.ShapeDtypeStruct((r, LANES), BF) for r in (ROWS_R, ROWS_C, ROWS_C)]
    return pl.pallas_call(
        pack_kernel,
        out_shape=shapes,
        in_specs=[VMEM] * 3,
        out_specs=[VMEM] * 3,
        compiler_params=pltpu.CompilerParams(vmem_limit_bytes=SMALL),
        name="pack",
    )(embeddings, margin.reshape(1, CPD), group.reshape(1, CPD))


TILE = 1024


def pair_kernel(n_r, n_c, n_sum, *refs):
    r_in, c_in, rest = refs[:n_r], refs[n_r : n_r + n_c], refs[n_r + n_c :]
    sums, outs = rest[:n_sum], rest[n_sum : n_sum + n_r]
    rbuf, rmeta, cbuf, cmeta, rm, rg, acc, r_sem, c_sem = rest[n_sum + n_r :]
    tiles = n_c // 2
    r_copies, c_copies = [], []
    at = 0
    for i, ref in enumerate(r_in):
        n = ref.shape[0]
        own = [
            pltpu.make_async_copy(
                ref.at[:, f * CPD : (f + 1) * CPD, :],
                rbuf.at[at : at + n, :, f * LANES : (f + 1) * LANES],
                r_sem.at[i, f],
            )
            for f in range(CHUNKS)
        ]
        own.append(pltpu.make_async_copy(ref.at[:, CHUNKS * CPD :, :], rmeta.at[at : at + n], r_sem.at[i, CHUNKS]))
        r_copies += own
        at += n

    def c_copy(ref, t, h):
        own = [
            pltpu.make_async_copy(
                ref.at[:, f * HALF : (f + 1) * HALF, :],
                cbuf.at[pl.ds(t * 8, 8), h * HALF : (h + 1) * HALF, f * LANES : (f + 1) * LANES],
                c_sem.at[t, h, f],
            )
            for f in range(CHUNKS)
        ]
        own.append(
            pltpu.make_async_copy(ref.at[:, CHUNKS * HALF :, :], cmeta.at[h, pl.ds(t * 8, 8)], c_sem.at[t, h, CHUNKS])
        )
        return own

    for c in r_copies:
        c.start()
    for t in range(tiles):
        for h in range(2):
            for c in c_copy(c_in[2 * t + h], t, h):
                c.start()
    for c in r_copies:
        c.wait()
    for k in range(at):
        m = rmeta[k].astype(F32)
        rm[k * CPD : (k + 1) * CPD, :] = jnp.broadcast_to(m[0:1] * 0.0005, (CPD, CPD)).T
        rg[k * CPD : (k + 1) * CPD, :] = jnp.broadcast_to(m[1:2], (CPD, CPD)).T
    if sums:
        o = 0
        for ref in sums:
            n = ref.shape[0]
            acc[o : o + n, :] = ref[...]
            o += n
    else:
        acc[...] = jnp.zeros_like(acc)
    lane = lax.broadcasted_iota(jnp.int32, (1, LANES), 1)

    def body(t, carry):
        for h in range(2):
            for c in c_copy(c_in[h], t, h):
                c.wait()
        ct = cbuf[pl.ds(t * 8, 8)].reshape(TILE, D)
        margins, groups = [], []
        for k in range(8):
            m0 = cmeta[0, t * 8 + k].astype(F32)
            m1 = cmeta[1, t * 8 + k].astype(F32)
            margins.append(jnp.where(lane < HALF, m0[0:1], m1[0:1]) * 0.0005)
            groups.append(jnp.where(lane < HALF, m0[1:2], m1[1:2]))
        for r0 in range(0, at * CPD, 256):
            rt = rbuf[r0 // CPD : r0 // CPD + 2].reshape(256, D)
            cos = lax.dot_general(rt, ct, (((1,), (1,)), ((), ())), preferred_element_type=F32)
            parts = []
            for k in range(8):
                over = jnp.maximum(cos[:, k * LANES : (k + 1) * LANES] - rm[r0 : r0 + 256, :] - margins[k], 0.0)
                parts.append(jnp.where(rg[r0 : r0 + 256, :] != groups[k], over, 0.0).astype(BF))
            s = jnp.concatenate(parts, axis=1)
            acc[r0 : r0 + 256, :] += jnp.dot(s, ct, preferred_element_type=F32)
        return carry

    lax.fori_loop(0, tiles, body, 0)
    o = 0
    for out in outs:
        n = out.shape[0]
        out[...] = acc[o : o + n, :].astype(out.dtype)
        o += n


def pair(r_in, c_in, out_dtype, sums=()):
    blocks = sum(a.shape[0] for a in r_in)
    rows, n_c = blocks * CPD, len(c_in)
    tiles = n_c // 2
    return pl.pallas_call(
        functools.partial(pair_kernel, len(r_in), n_c, len(sums)),
        out_shape=[jax.ShapeDtypeStruct((a.shape[0] * CPD, D), out_dtype) for a in r_in],
        in_specs=[ANY] * (len(r_in) + n_c) + [VMEM] * len(sums),
        out_specs=[VMEM] * len(r_in),
        scratch_shapes=[
            pltpu.VMEM((blocks, CPD, D), BF),
            pltpu.VMEM((blocks, META, LANES), BF),
            pltpu.VMEM((tiles * 8, CPD, D), BF),
            pltpu.VMEM((2, tiles * 8, META, LANES), BF),
            pltpu.VMEM((rows, CPD), F32),
            pltpu.VMEM((rows, CPD), F32),
            pltpu.VMEM((rows, D), F32),
            pltpu.SemaphoreType.DMA((len(r_in), CHUNKS + 1)),
            pltpu.SemaphoreType.DMA((tiles, 2, CHUNKS + 1)),
        ],
        compiler_params=pltpu.CompilerParams(vmem_limit_bytes=20 << 20),
        cost_estimate=pl.CostEstimate(
            flops=4 * rows * tiles * TILE * D, bytes_accessed=(tiles * TILE + rows) * D * 2, transcendentals=0
        ),
        name="pair",
    )(*r_in, *c_in, *sums)


def join_kernel(pieces, n_in, *refs):
    ins, outs, sem = refs[:n_in], refs[n_in:-1], refs[-1]
    copies = []
    for out, (i, j) in zip(outs, pieces, strict=True):
        n = ins[i].shape[0]
        copies.append((ins[i], out.at[:n]))
        copies.append((ins[j], out.at[n:]))
    copies = [pltpu.make_async_copy(src, dst, sem.at[k]) for k, (src, dst) in enumerate(copies)]
    for c in copies:
        c.start()
    for c in copies:
        c.wait()


def join(pieces, *ins):
    return pl.pallas_call(
        functools.partial(join_kernel, pieces, len(ins)),
        out_shape=[jax.ShapeDtypeStruct((ins[i].shape[0] + ins[j].shape[0], LANES), BF) for i, j in pieces],
        in_specs=[ANY] * len(ins),
        out_specs=[VMEM] * len(pieces),
        scratch_shapes=[pltpu.SemaphoreType.DMA((2 * len(pieces),))],
        compiler_params=pltpu.CompilerParams(vmem_limit_bytes=SMALL),
        name="join",
    )(*ins)


def final_kernel(rate, emb, own, arrived, out):
    e = emb[...]
    lengths = jnp.sqrt(jnp.sum(e * e, axis=1, keepdims=True) + 1e-06)
    unit = e / lengths
    grad = 4.0 * (own[...] + arrived[...].astype(F32))
    radial = jnp.sum(unit * grad, axis=1, keepdims=True)
    out[...] = e - rate * ((grad - unit * radial) / lengths)


def per_device(embeddings, margin, group):
    classes = embeddings.shape[0] * lax.axis_size("row") * lax.axis_size("col")
    whole, first, second = pack(embeddings, margin, group)

    def round_xy(s, a, b):
        return swap(a, RING[s], RING[(s + 1) % 4]), swap(b, RING[(s + 2) % 4], RING[(s + 3) % 4])

    z = swap(whole, "za", "zb")
    ra, rb = round_xy(0, first, second)
    z1, a, b = join(((0, 1), (2, 3), (4, 5)), whole, z, first, ra, second, rb)
    z2 = swap(z1, "zb", "za")
    ra, rb = round_xy(1, a, b)
    a, b = join(((0, 1), (2, 3)), a, ra, b, rb, z2)
    z3 = swap(z2, "za", "zb")
    ra, rb = round_xy(2, a, b)
    a0, b0 = join(((0, 1), (2, 3)), a, ra, b, rb, z3)
    z4 = swap(z3, "zb", "za")
    a1, b1 = round_xy(3, a0, b0)

    def cols(*arrays):
        return [v.reshape(-1, ROWS_C, LANES) for v in arrays]

    early = cols(a0, b0, swap_cores(a0), swap_cores(b0))
    z1, z2, z3, z4 = (v.reshape(-1, ROWS_R, LANES) for v in (z1, z2, z3, z4))
    p1, p2, p3 = pair([z1, z2, z3], early, F32)
    z4, a1, b1, p1, p2, p3 = lax.optimization_barrier((z4, a1, b1, p1, p2, p3))
    late = cols(a1, b1, swap_cores(a1), swap_cores(b1))
    (p4,) = pair([z4], early, F32)
    (p4,) = pair([z4], late, BF, [p4])
    q = swap(p4, "zb", "za")
    p1, p2, p3 = pair([z1, z2, z3], late, F32, [p1, p2, p3])
    q = swap((p3 + q).astype(BF), "za", "zb")
    q = swap((p2 + q).astype(BF), "zb", "za")
    own = p1 + q
    q = swap(own[CPD:].astype(BF), "za", "zb")

    rate = D * math.sqrt(D) / (3.0 * math.sqrt(classes))
    return pl.pallas_call(
        functools.partial(final_kernel, rate),
        out_shape=jax.ShapeDtypeStruct((CPD, D), F32),
        in_specs=[VMEM] * 3,
        out_specs=VMEM,
        compiler_params=pltpu.CompilerParams(vmem_limit_bytes=SMALL),
        name="final",
    )(embeddings, own[:CPD], q)


def solution(mesh):
    in_specs = (P(("row", "col"), None), P(("row", "col")), P(("row", "col")))
    out_specs = P(("row", "col"), None)
    return jax.shard_map(per_device, mesh=mesh, in_specs=in_specs, out_specs=out_specs, check_vma=False)
```

```python
import functools
import itertools
import math

import jax
import jax.numpy as jnp
from jax import lax
from jax.experimental import pallas as pl
from jax.experimental.pallas import tpu as pltpu
from jax.sharding import PartitionSpec as P

BF = jnp.bfloat16
F32 = jnp.float32
D = 512
CPD = 128
META = 16
LANES = 128
CHUNKS = D // LANES
PACKED = CHUNKS * CPD + META
SMALL = 6 << 20
AXES = ("row", "col")
VMEM = pl.BlockSpec(memory_space=pltpu.VMEM)
ANY = pl.BlockSpec(memory_space=pl.ANY)


def _flat(x, y, z, core):
    return ((((z // 2) * 4 + x) * 2 + z % 2) * 4 + y) * 2 + core


LINKS = {
    "xa": lambda x, y, z: (x ^ 1, y, z),
    "xb": lambda x, y, z: (3 - x, y, z),
    "xaya": lambda x, y, z: (x ^ 1, y ^ 1, z),
    "xbyb": lambda x, y, z: (3 - x, 3 - y, z),
    "ya": lambda x, y, z: (x, y ^ 1, z),
    "yb": lambda x, y, z: (x, 3 - y, z),
    "za": lambda x, y, z: (x, y, z ^ 1),
    "zb": lambda x, y, z: (x, y, (z - 1) % 8 if z % 2 == 0 else (z + 1) % 8),
}


def swap(block, link0, link1):
    pairs = []
    for x, y, z, core in itertools.product(range(4), range(4), range(8), range(2)):
        pairs.append((_flat(x, y, z, core), _flat(*LINKS[(link0, link1)[core]](x, y, z), core)))
    return lax.ppermute(block, AXES, pairs)


def shift(block, sign):
    pairs = []
    for x, y, z, core in itertools.product(range(4), range(4), range(8), range(2)):
        step = 2 * sign * (1 if (z + core) % 2 == 0 else -1)
        pairs.append((_flat(x, y, z, core), _flat(x, y, (z + step) % 8, core)))
    return lax.ppermute(block, AXES, pairs)


def swap_cores(block):
    return lax.ppermute(block, AXES, [(i, i ^ 1) for i in range(256)])


def pack_kernel(emb, margin, group, whole):
    e = emb[...]
    unit = (e / jnp.sqrt(jnp.sum(e * e, axis=1, keepdims=True) + 1e-06)).astype(BF)
    row = lax.broadcasted_iota(jnp.int32, (META, LANES), 0)
    meta = jnp.where(row == 0, margin[...], jnp.where(row == 1, group[...], 0)).astype(F32).astype(BF)
    for f in range(CHUNKS):
        whole[f * CPD : (f + 1) * CPD, :] = unit[:, f * LANES : (f + 1) * LANES]
    whole[CHUNKS * CPD :, :] = meta


def pack(embeddings, margin, group):
    return pl.pallas_call(
        pack_kernel,
        out_shape=jax.ShapeDtypeStruct((PACKED, LANES), BF),
        in_specs=[VMEM] * 3,
        out_specs=VMEM,
        compiler_params=pltpu.CompilerParams(vmem_limit_bytes=SMALL),
        name="pack",
    )(embeddings, margin.reshape(1, CPD), group.reshape(1, CPD))


TILE = 1024
TB = TILE // CPD


def pair_kernel(n_r, n_c, n_sum, *refs):
    r_in, c_in, rest = refs[:n_r], refs[n_r : n_r + n_c], refs[n_r + n_c :]
    sums, outs = rest[:n_sum], rest[n_sum : n_sum + n_r]
    rbuf, rmeta, cbuf, cmeta, rm, rg, acc, r_sem, c_sem = rest[n_sum + n_r :]

    def unpack(ref, buf, meta, at, sems):
        n = ref.shape[0]
        own = [
            pltpu.make_async_copy(
                ref.at[:, f * CPD : (f + 1) * CPD, :],
                buf.at[at : at + n, :, f * LANES : (f + 1) * LANES],
                sems(f),
            )
            for f in range(CHUNKS)
        ]
        own.append(pltpu.make_async_copy(ref.at[:, CHUNKS * CPD :, :], meta.at[at : at + n], sems(CHUNKS)))
        return own

    copies, waits, at = [], {}, 0
    for i, ref in enumerate(r_in):
        copies += unpack(ref, rbuf, rmeta, at, lambda f, i=i: r_sem.at[i, f])
        at += ref.shape[0]
    col = 0
    for i, ref in enumerate(c_in):
        own = unpack(ref, cbuf, cmeta, col, lambda f, i=i: c_sem.at[i, f])
        waits.setdefault(col // TB, []).extend(own)
        col += ref.shape[0]
    for c in copies + sum(waits.values(), []):
        c.start()
    for c in copies:
        c.wait()
    for k in range(at):
        m = rmeta[k].astype(F32)
        rm[k * CPD : (k + 1) * CPD, :] = jnp.broadcast_to(m[0:1] * 0.0005, (CPD, CPD)).T
        rg[k * CPD : (k + 1) * CPD, :] = jnp.broadcast_to(m[1:2], (CPD, CPD)).T
    if sums:
        o = 0
        for ref in sums:
            n = ref.shape[0]
            acc[o : o + n, :] = ref[...]
            o += n
    else:
        acc[...] = jnp.zeros_like(acc)
    for t in range(col // TB):
        for c in waits[t]:
            c.wait()

    def body(t, carry):
        ct = cbuf[pl.ds(t * TB, TB)].reshape(TILE, D)
        margins, groups = [], []
        for k in range(TB):
            m = cmeta[t * TB + k].astype(F32)
            margins.append(m[0:1] * 0.0005)
            groups.append(m[1:2])
        for r0 in range(0, at * CPD, 256):
            rt = rbuf[r0 // CPD : r0 // CPD + 2].reshape(256, D)
            cos = lax.dot_general(rt, ct, (((1,), (1,)), ((), ())), preferred_element_type=F32)
            parts = []
            for k in range(TB):
                over = jnp.maximum(cos[:, k * LANES : (k + 1) * LANES] - rm[r0 : r0 + 256, :] - margins[k], 0.0)
                parts.append(jnp.where(rg[r0 : r0 + 256, :] != groups[k], over, 0.0).astype(BF))
            s = jnp.concatenate(parts, axis=1)
            acc[r0 : r0 + 256, :] += jnp.dot(s, ct, preferred_element_type=F32)
        return carry

    lax.fori_loop(0, col // TB, body, 0)
    o = 0
    for out in outs:
        n = out.shape[0]
        out[...] = acc[o : o + n, :].astype(out.dtype)
        o += n


def pair(r_in, c_in, out_dtype, sums=()):
    r_in, c_in = ([a.reshape(-1, PACKED, LANES) for a in v] for v in (r_in, c_in))
    r_blocks, c_blocks = (sum(a.shape[0] for a in v) for v in (r_in, c_in))
    rows, n_c = r_blocks * CPD, len(c_in)
    return pl.pallas_call(
        functools.partial(pair_kernel, len(r_in), n_c, len(sums)),
        out_shape=[jax.ShapeDtypeStruct((a.shape[0] * CPD, D), out_dtype) for a in r_in],
        in_specs=[ANY] * (len(r_in) + n_c) + [VMEM] * len(sums),
        out_specs=[VMEM] * len(r_in),
        scratch_shapes=[
            pltpu.VMEM((r_blocks, CPD, D), BF),
            pltpu.VMEM((r_blocks, META, LANES), BF),
            pltpu.VMEM((c_blocks, CPD, D), BF),
            pltpu.VMEM((c_blocks, META, LANES), BF),
            pltpu.VMEM((rows, CPD), F32),
            pltpu.VMEM((rows, CPD), F32),
            pltpu.VMEM((rows, D), F32),
            pltpu.SemaphoreType.DMA((len(r_in), CHUNKS + 1)),
            pltpu.SemaphoreType.DMA((n_c, CHUNKS + 1)),
        ],
        compiler_params=pltpu.CompilerParams(vmem_limit_bytes=20 << 20),
        cost_estimate=pl.CostEstimate(
            flops=4 * rows * c_blocks * CPD * D, bytes_accessed=(c_blocks * CPD + rows) * D * 2, transcendentals=0
        ),
        name="pair",
    )(*r_in, *c_in, *sums)


def join_kernel(pieces, n_in, *refs):
    ins, outs, sem = refs[:n_in], refs[n_in:-1], refs[-1]
    copies = []
    for out, which in zip(outs, pieces, strict=True):
        at = 0
        for i in which:
            n = ins[i].shape[0]
            copies.append(pltpu.make_async_copy(ins[i], out.at[at : at + n], sem.at[len(copies)]))
            at += n
    for c in copies:
        c.start()
    for c in copies:
        c.wait()


def join(pieces, *ins):
    return pl.pallas_call(
        functools.partial(join_kernel, pieces, len(ins)),
        out_shape=[jax.ShapeDtypeStruct((sum(ins[i].shape[0] for i in p), LANES), BF) for p in pieces],
        in_specs=[ANY] * len(ins),
        out_specs=[VMEM] * len(pieces),
        scratch_shapes=[pltpu.SemaphoreType.DMA((sum(map(len, pieces)),))],
        compiler_params=pltpu.CompilerParams(vmem_limit_bytes=SMALL),
        name="join",
    )(*ins)


def final_kernel(rate, emb, own, *refs):
    arrived, out = refs[:-1], refs[-1]
    e = emb[...]
    lengths = jnp.sqrt(jnp.sum(e * e, axis=1, keepdims=True) + 1e-06)
    unit = e / lengths
    grad = 4.0 * sum((ref[...].astype(F32) for ref in arrived), own[...])
    radial = jnp.sum(unit * grad, axis=1, keepdims=True)
    out[...] = e - rate * ((grad - unit * radial) / lengths)


def per_device(embeddings, margin, group):
    classes = embeddings.shape[0] * lax.axis_size("row") * lax.axis_size("col")
    whole = pack(embeddings, margin, group)

    near = swap(whole, "za", "zb")
    square = [swap(whole, a, b) for a, b in (("xa", "xb"), ("ya", "yb"), ("xaya", "xbyb"))]
    both, c0 = join(((0, 1), (0, 2, 3, 4)), whole, near, *square)
    back = swap(both, "zb", "za")
    c3, c1, c2 = (swap(c0, b, a) for a, b in (("xaya", "xbyb"), ("xa", "xb"), ("ya", "yb")))
    ahead = swap(back, "za", "zb")
    far = swap(ahead, "zb", "za")
    e0, e1 = swap_cores(c0), swap_cores(c1)
    sums = pair([ahead, back, both], [c0, e0, c1, e1], F32)
    far, c2, c3, *sums = lax.optimization_barrier((far, c2, c3, *sums))
    e2, e3 = swap_cores(c2), swap_cores(c3)
    (p_far,) = pair([far], [c0, e0, c1, e1], F32)
    (p_far,) = pair([far], [c2, e2, c3, e3], BF, [p_far])
    q = swap(p_far, "zb", "za")
    p_ahead, p_back, p_own = pair([ahead, back, both], [c2, e2, c3, e3], F32, sums)
    q_near = swap(p_own[CPD:].astype(BF), "za", "zb")
    q = swap((p_ahead + q).astype(BF), "za", "zb")
    p_back = (p_back + q).astype(BF)
    arrived = (q_near, swap(p_back[:CPD], "zb", "za"), shift(p_back[CPD:], -1))

    rate = D * math.sqrt(D) / (3.0 * math.sqrt(classes))
    return pl.pallas_call(
        functools.partial(final_kernel, rate),
        out_shape=jax.ShapeDtypeStruct((CPD, D), F32),
        in_specs=[VMEM] * 5,
        out_specs=VMEM,
        compiler_params=pltpu.CompilerParams(vmem_limit_bytes=SMALL),
        name="final",
    )(embeddings, p_own[:CPD], *arrived)


def solution(mesh):
    in_specs = (P(("row", "col"), None), P(("row", "col")), P(("row", "col")))
    out_specs = P(("row", "col"), None)
    return jax.shard_map(per_device, mesh=mesh, in_specs=in_specs, out_specs=out_specs, check_vma=False)
```

```python
import functools
import itertools
import math

import jax
import jax.numpy as jnp
from jax import lax
from jax.experimental import pallas as pl
from jax.experimental.pallas import tpu as pltpu
from jax.sharding import PartitionSpec as P

BF = jnp.bfloat16
F32 = jnp.float32
D = 512
CPD = 128
META = 16
LANES = 128
CHUNKS = D // LANES
PACKED = CHUNKS * CPD + META
SMALL = 6 << 20
AXES = ("row", "col")
VMEM = pl.BlockSpec(memory_space=pltpu.VMEM)
ANY = pl.BlockSpec(memory_space=pl.ANY)


def _flat(x, y, z, core):
    return ((((z // 2) * 4 + x) * 2 + z % 2) * 4 + y) * 2 + core


LINKS = {
    "xa": lambda x, y, z: (x ^ 1, y, z),
    "xb": lambda x, y, z: (3 - x, y, z),
    "xaya": lambda x, y, z: (x ^ 1, y ^ 1, z),
    "xbyb": lambda x, y, z: (3 - x, 3 - y, z),
    "ya": lambda x, y, z: (x, y ^ 1, z),
    "yb": lambda x, y, z: (x, 3 - y, z),
    "za": lambda x, y, z: (x, y, z ^ 1),
    "zb": lambda x, y, z: (x, y, (z - 1) % 8 if z % 2 == 0 else (z + 1) % 8),
}


def swap(block, link0, link1):
    pairs = []
    for x, y, z, core in itertools.product(range(4), range(4), range(8), range(2)):
        pairs.append((_flat(x, y, z, core), _flat(*LINKS[(link0, link1)[core]](x, y, z), core)))
    return lax.ppermute(block, AXES, pairs)


def shift(block, sign):
    pairs = []
    for x, y, z, core in itertools.product(range(4), range(4), range(8), range(2)):
        step = 2 * sign * (1 if (z + core) % 2 == 0 else -1)
        pairs.append((_flat(x, y, z, core), _flat(x, y, (z + step) % 8, core)))
    return lax.ppermute(block, AXES, pairs)


def swap_cores(block):
    return lax.ppermute(block, AXES, [(i, i ^ 1) for i in range(256)])


def pack_kernel(emb, margin, group, whole):
    e = emb[...]
    unit = (e / jnp.sqrt(jnp.sum(e * e, axis=1, keepdims=True) + 1e-06)).astype(BF)
    row = lax.broadcasted_iota(jnp.int32, (META, LANES), 0)
    meta = jnp.where(row == 0, margin[...], jnp.where(row == 1, group[...], 0)).astype(F32).astype(BF)
    for f in range(CHUNKS):
        whole[f * CPD : (f + 1) * CPD, :] = unit[:, f * LANES : (f + 1) * LANES]
    whole[CHUNKS * CPD :, :] = meta


def pack(embeddings, margin, group):
    return pl.pallas_call(
        pack_kernel,
        out_shape=jax.ShapeDtypeStruct((PACKED, LANES), BF),
        in_specs=[VMEM] * 3,
        out_specs=VMEM,
        compiler_params=pltpu.CompilerParams(vmem_limit_bytes=SMALL),
        name="pack",
    )(embeddings, margin.reshape(1, CPD), group.reshape(1, CPD))


TILE = 1024
TB = TILE // CPD


def pair_kernel(n_r, n_c, n_sum, *refs):
    r_in, c_in, rest = refs[:n_r], refs[n_r : n_r + n_c], refs[n_r + n_c :]
    sums, outs = rest[:n_sum], rest[n_sum : n_sum + n_r]
    rbuf, rmeta, cbuf, cmeta, rm, rg, acc, r_sem, c_sem = rest[n_sum + n_r :]

    def unpack(ref, buf, meta, at, sems):
        n = ref.shape[0]
        own = [
            pltpu.make_async_copy(
                ref.at[:, f * CPD : (f + 1) * CPD, :],
                buf.at[at : at + n, :, f * LANES : (f + 1) * LANES],
                sems(f),
            )
            for f in range(CHUNKS)
        ]
        own.append(pltpu.make_async_copy(ref.at[:, CHUNKS * CPD :, :], meta.at[at : at + n], sems(CHUNKS)))
        return own

    copies, waits, at = [], {}, 0
    for i, ref in enumerate(r_in):
        copies += unpack(ref, rbuf, rmeta, at, lambda f, i=i: r_sem.at[i, f])
        at += ref.shape[0]
    col = 0
    for i, ref in enumerate(c_in):
        own = unpack(ref, cbuf, cmeta, col, lambda f, i=i: c_sem.at[i, f])
        waits.setdefault(col // TB, []).extend(own)
        col += ref.shape[0]
    for c in copies + sum(waits.values(), []):
        c.start()
    for c in copies:
        c.wait()
    for k in range(at):
        m = rmeta[k].astype(F32)
        rm[k * CPD : (k + 1) * CPD, :] = jnp.broadcast_to(m[0:1] * 0.0005, (CPD, CPD)).T
        rg[k * CPD : (k + 1) * CPD, :] = jnp.broadcast_to(m[1:2], (CPD, CPD)).T
    if sums:
        o = 0
        for ref in sums:
            n = ref.shape[0]
            acc[o : o + n, :] = ref[...]
            o += n
    else:
        acc[...] = jnp.zeros_like(acc)
    for t in range(col // TB):
        for c in waits[t]:
            c.wait()

    def body(t, carry):
        ct = cbuf[pl.ds(t * TB, TB)].reshape(TILE, D)
        margins, groups = [], []
        for k in range(TB):
            m = cmeta[t * TB + k].astype(F32)
            margins.append(m[0:1] * 0.0005)
            groups.append(m[1:2])
        for r0 in range(0, at * CPD, 256):
            rt = rbuf[r0 // CPD : r0 // CPD + 2].reshape(256, D)
            cos = lax.dot_general(rt, ct, (((1,), (1,)), ((), ())), preferred_element_type=F32)
            parts = []
            for k in range(TB):
                over = jnp.maximum(cos[:, k * LANES : (k + 1) * LANES] - rm[r0 : r0 + 256, :] - margins[k], 0.0)
                parts.append(jnp.where(rg[r0 : r0 + 256, :] != groups[k], over, 0.0).astype(BF))
            s = jnp.concatenate(parts, axis=1)
            acc[r0 : r0 + 256, :] += jnp.dot(s, ct, preferred_element_type=F32)
        return carry

    lax.fori_loop(0, col // TB, body, 0)
    o = 0
    for out in outs:
        n = out.shape[0]
        out[...] = acc[o : o + n, :].astype(out.dtype)
        o += n


def pair(r_in, c_in, out_dtype, sums=(), weight=1.0):
    r_in, c_in = ([a.reshape(-1, PACKED, LANES) for a in v] for v in (r_in, c_in))
    r_blocks, c_blocks = (sum(a.shape[0] for a in v) for v in (r_in, c_in))
    rows, n_c = r_blocks * CPD, len(c_in)
    return pl.pallas_call(
        functools.partial(pair_kernel, len(r_in), n_c, len(sums)),
        out_shape=[jax.ShapeDtypeStruct((a.shape[0] * CPD, D), out_dtype) for a in r_in],
        in_specs=[ANY] * (len(r_in) + n_c) + [VMEM] * len(sums),
        out_specs=[VMEM] * len(r_in),
        scratch_shapes=[
            pltpu.VMEM((r_blocks, CPD, D), BF),
            pltpu.VMEM((r_blocks, META, LANES), BF),
            pltpu.VMEM((c_blocks, CPD, D), BF),
            pltpu.VMEM((c_blocks, META, LANES), BF),
            pltpu.VMEM((rows, CPD), F32),
            pltpu.VMEM((rows, CPD), F32),
            pltpu.VMEM((rows, D), F32),
            pltpu.SemaphoreType.DMA((len(r_in), CHUNKS + 1)),
            pltpu.SemaphoreType.DMA((n_c, CHUNKS + 1)),
        ],
        compiler_params=pltpu.CompilerParams(vmem_limit_bytes=20 << 20),
        cost_estimate=pl.CostEstimate(
            flops=int(weight * 4 * rows * c_blocks * CPD * D),
            bytes_accessed=int(weight * (c_blocks * CPD + rows) * D * 2), transcendentals=0
        ),
        name="pair",
    )(*r_in, *c_in, *sums)


def join_kernel(pieces, n_in, *refs):
    ins, outs, sem = refs[:n_in], refs[n_in:-1], refs[-1]
    copies = []
    for out, which in zip(outs, pieces, strict=True):
        at = 0
        for i in which:
            n = ins[i].shape[0]
            copies.append(pltpu.make_async_copy(ins[i], out.at[at : at + n], sem.at[len(copies)]))
            at += n
    for c in copies:
        c.start()
    for c in copies:
        c.wait()


def join(pieces, *ins):
    return pl.pallas_call(
        functools.partial(join_kernel, pieces, len(ins)),
        out_shape=[jax.ShapeDtypeStruct((sum(ins[i].shape[0] for i in p), LANES), BF) for p in pieces],
        in_specs=[ANY] * len(ins),
        out_specs=[VMEM] * len(pieces),
        scratch_shapes=[pltpu.SemaphoreType.DMA((sum(map(len, pieces)),))],
        compiler_params=pltpu.CompilerParams(vmem_limit_bytes=SMALL),
        name="join",
    )(*ins)


def final_kernel(rate, emb, own, *refs):
    arrived, out = refs[:-1], refs[-1]
    e = emb[...]
    lengths = jnp.sqrt(jnp.sum(e * e, axis=1, keepdims=True) + 1e-06)
    unit = e / lengths
    grad = 4.0 * sum((ref[...].astype(F32) for ref in arrived), own[...])
    radial = jnp.sum(unit * grad, axis=1, keepdims=True)
    out[...] = e - rate * ((grad - unit * radial) / lengths)


def per_device(embeddings, margin, group):
    classes = embeddings.shape[0] * lax.axis_size("row") * lax.axis_size("col")
    whole = pack(embeddings, margin, group)

    near = swap(whole, "za", "zb")
    square = [swap(whole, a, b) for a, b in (("xa", "xb"), ("ya", "yb"), ("xaya", "xbyb"))]
    (both,) = join(((0, 1),), whole, near)
    back = swap(both, "zb", "za")
    (c0,) = join(((0, 1, 2, 3),), whole, *square)
    far, ahead = shift(back, 1), swap(back, "za", "zb")
    c3, c1, c2 = (swap(c0, b, a) for a, b in (("xaya", "xbyb"), ("xa", "xb"), ("ya", "yb")))
    e0 = swap_cores(c0)
    far, ahead, c1, c2, c3 = lax.optimization_barrier((far, ahead, c1, c2, c3))
    e1, e2, e3 = swap_cores(c1), swap_cores(c2), swap_cores(c3)
    cols = [c0, c1, c2, c3, e0, e1, e2, e3]
    (p_far,) = pair([far], cols[:4], F32)
    (p_far,) = pair([far], cols[4:], BF, [p_far])
    q = swap(p_far, "zb", "za")
    p_ahead, p_own = pair([ahead, both], cols, F32)
    q_near = swap(p_own[CPD:].astype(BF), "za", "zb")
    q = swap((p_ahead + q).astype(BF), "za", "zb")
    (p_back,) = pair([back], cols, F32)
    p_back = (p_back + q).astype(BF)
    arrived = (q_near, swap(p_back[:CPD], "zb", "za"), shift(p_back[CPD:], -1))

    rate = D * math.sqrt(D) / (3.0 * math.sqrt(classes))
    return pl.pallas_call(
        functools.partial(final_kernel, rate),
        out_shape=jax.ShapeDtypeStruct((CPD, D), F32),
        in_specs=[VMEM] * 5,
        out_specs=VMEM,
        compiler_params=pltpu.CompilerParams(vmem_limit_bytes=SMALL),
        name="final",
    )(embeddings, p_own[:CPD], *arrived)


def solution(mesh):
    in_specs = (P(("row", "col"), None), P(("row", "col")), P(("row", "col")))
    out_specs = P(("row", "col"), None)
    return jax.shard_map(per_device, mesh=mesh, in_specs=in_specs, out_specs=out_specs, check_vma=False)
```

```python
import functools
import itertools
import math

import jax
import jax.numpy as jnp
from jax import lax
from jax.experimental import pallas as pl
from jax.experimental.pallas import tpu as pltpu
from jax.sharding import PartitionSpec as P

BF = jnp.bfloat16
F32 = jnp.float32
D = 512
CPD = 128
META = 16
LANES = 128
CHUNKS = D // LANES
PACKED = CHUNKS * CPD + META
SMALL = 6 << 20
AXES = ("row", "col")
VMEM = pl.BlockSpec(memory_space=pltpu.VMEM)
ANY = pl.BlockSpec(memory_space=pl.ANY)


def _flat(x, y, z, core):
    return ((((z // 2) * 4 + x) * 2 + z % 2) * 4 + y) * 2 + core


LINKS = {
    "xa": lambda x, y, z: (x ^ 1, y, z),
    "xb": lambda x, y, z: (3 - x, y, z),
    "xaya": lambda x, y, z: (x ^ 1, y ^ 1, z),
    "xbyb": lambda x, y, z: (3 - x, 3 - y, z),
    "ya": lambda x, y, z: (x, y ^ 1, z),
    "yb": lambda x, y, z: (x, 3 - y, z),
    "za": lambda x, y, z: (x, y, z ^ 1),
    "zb": lambda x, y, z: (x, y, (z - 1) % 8 if z % 2 == 0 else (z + 1) % 8),
}


def swap(block, link0, link1):
    pairs = []
    for x, y, z, core in itertools.product(range(4), range(4), range(8), range(2)):
        pairs.append((_flat(x, y, z, core), _flat(*LINKS[(link0, link1)[core]](x, y, z), core)))
    return lax.ppermute(block, AXES, pairs)


def shift(block, sign):
    pairs = []
    for x, y, z, core in itertools.product(range(4), range(4), range(8), range(2)):
        step = 2 * sign * (1 if (z + core) % 2 == 0 else -1)
        pairs.append((_flat(x, y, z, core), _flat(x, y, (z + step) % 8, core)))
    return lax.ppermute(block, AXES, pairs)


def swap_cores(block):
    return lax.ppermute(block, AXES, [(i, i ^ 1) for i in range(256)])


def pack_kernel(emb_hbm, margin_hbm, group_hbm, whole, emb, margin, group, sem):
    pairs = ((emb_hbm, emb), (margin_hbm, margin), (group_hbm, group))
    copies = [pltpu.make_async_copy(src, dst, sem.at[i]) for i, (src, dst) in enumerate(pairs)]
    for c in copies:
        c.start()
    for c in copies:
        c.wait()
    e = emb[...]
    unit = (e / jnp.sqrt(jnp.sum(e * e, axis=1, keepdims=True) + 1e-06)).astype(BF)
    row = lax.broadcasted_iota(jnp.int32, (META, LANES), 0)
    meta = jnp.where(row == 0, margin[...], jnp.where(row == 1, group[...], 0)).astype(F32).astype(BF)
    for f in range(CHUNKS):
        whole[f * CPD : (f + 1) * CPD, :] = unit[:, f * LANES : (f + 1) * LANES]
    whole[CHUNKS * CPD :, :] = meta


def pack(embeddings, margin, group):
    return pl.pallas_call(
        pack_kernel,
        out_shape=jax.ShapeDtypeStruct((PACKED, LANES), BF),
        in_specs=[pl.BlockSpec(memory_space=pltpu.HBM)] * 3,
        out_specs=VMEM,
        scratch_shapes=[
            pltpu.VMEM((CPD, D), F32),
            pltpu.VMEM((1, CPD), jnp.int32),
            pltpu.VMEM((1, CPD), jnp.int32),
            pltpu.SemaphoreType.DMA((3,)),
        ],
        compiler_params=pltpu.CompilerParams(vmem_limit_bytes=SMALL),
        name="pack",
    )(embeddings, margin.reshape(1, CPD), group.reshape(1, CPD))


TB = 8


def units(ref, k):
    return jnp.concatenate([ref[k, f * CPD : (f + 1) * CPD, :] for f in range(CHUNKS)], axis=1)


def pair_kernel(n_r, n_c, n_sum, *refs):
    r_in, c_in, rest = refs[:n_r], refs[n_r : n_r + n_c], refs[n_r + n_c :]
    sums, outs = rest[:n_sum], rest[n_sum:]
    r_blocks, c_blocks = ([(ref, k) for ref in v for k in range(ref.shape[0])] for v in (r_in, c_in))
    acc, r_margin, r_group = [], [], []
    for i in range(0, len(r_blocks), 2):
        meta = [ref[k, CHUNKS * CPD :, :].astype(F32) for ref, k in r_blocks[i : i + 2]]
        r_margin.append(jnp.concatenate([jnp.broadcast_to(m[0:1] * 0.0005, (CPD, CPD)).T for m in meta], axis=0))
        r_group.append(jnp.concatenate([jnp.broadcast_to(m[1:2], (CPD, CPD)).T for m in meta], axis=0))
        acc.append(None)
    halves = [(ref, o) for ref in sums for o in range(0, ref.shape[0], 2 * CPD)]
    for i, (ref, o) in enumerate(halves):
        acc[i] = ref[o : o + 2 * CPD, :]
    for t in range(0, len(c_blocks), TB):
        tile = c_blocks[t : t + TB]
        meta = [ref[k, CHUNKS * CPD :, :].astype(F32) for ref, k in tile]
        ct = jnp.concatenate([units(ref, k) for ref, k in tile], axis=0)
        for i in range(len(acc)):
            rt = jnp.concatenate([units(ref, k) for ref, k in r_blocks[2 * i : 2 * i + 2]], axis=0)
            cos = lax.dot_general(rt, ct, (((1,), (1,)), ((), ())), preferred_element_type=F32)
            parts = []
            for k, m in enumerate(meta):
                over = jnp.maximum(cos[:, k * LANES : (k + 1) * LANES] - r_margin[i] - m[0:1] * 0.0005, 0.0)
                parts.append(jnp.where(r_group[i] != m[1:2], over, 0.0).astype(BF))
            part = jnp.dot(jnp.concatenate(parts, axis=1), ct, preferred_element_type=F32)
            acc[i] = part if acc[i] is None else acc[i] + part
    halves = [(ref, o) for ref in outs for o in range(0, ref.shape[0], 2 * CPD)]
    for i, (ref, o) in enumerate(halves):
        ref[o : o + 2 * CPD, :] = acc[i].astype(ref.dtype)


def pair(r_in, c_in, out_dtype, sums=()):
    r_in, c_in = ([a.reshape(-1, PACKED, LANES) for a in v] for v in (r_in, c_in))
    rows, cols = (sum(a.shape[0] for a in v) * CPD for v in (r_in, c_in))
    return pl.pallas_call(
        functools.partial(pair_kernel, len(r_in), len(c_in), len(sums)),
        out_shape=[jax.ShapeDtypeStruct((a.shape[0] * CPD, D), out_dtype) for a in r_in],
        in_specs=[VMEM] * (len(r_in) + len(c_in) + len(sums)),
        out_specs=[VMEM] * len(r_in),
        compiler_params=pltpu.CompilerParams(vmem_limit_bytes=20 << 20),
        cost_estimate=pl.CostEstimate(
            flops=4 * rows * cols * D, bytes_accessed=(cols + rows) * D * 2, transcendentals=0
        ),
        name="pair",
    )(*r_in, *c_in, *sums)


def join_kernel(pieces, n_in, *refs):
    ins, outs, sem = refs[:n_in], refs[n_in:-1], refs[-1]
    copies = []
    for out, which in zip(outs, pieces, strict=True):
        at = 0
        for i in which:
            n = ins[i].shape[0]
            copies.append(pltpu.make_async_copy(ins[i], out.at[at : at + n], sem.at[len(copies)]))
            at += n
    for c in copies:
        c.start()
    for c in copies:
        c.wait()


def join(pieces, *ins):
    return pl.pallas_call(
        functools.partial(join_kernel, pieces, len(ins)),
        out_shape=[jax.ShapeDtypeStruct((sum(ins[i].shape[0] for i in p), LANES), BF) for p in pieces],
        in_specs=[ANY] * len(ins),
        out_specs=[VMEM] * len(pieces),
        scratch_shapes=[pltpu.SemaphoreType.DMA((sum(map(len, pieces)),))],
        compiler_params=pltpu.CompilerParams(vmem_limit_bytes=SMALL),
        name="join",
    )(*ins)


def final_kernel(rate, emb, own, *refs):
    arrived, out = refs[:-1], refs[-1]
    e = emb[...]
    lengths = jnp.sqrt(jnp.sum(e * e, axis=1, keepdims=True) + 1e-06)
    unit = e / lengths
    grad = 4.0 * sum((ref[...].astype(F32) for ref in arrived), own[...])
    radial = jnp.sum(unit * grad, axis=1, keepdims=True)
    out[...] = e - rate * ((grad - unit * radial) / lengths)


def per_device(embeddings, margin, group):
    classes = embeddings.shape[0] * lax.axis_size("row") * lax.axis_size("col")
    whole = pack(embeddings, margin, group)

    near = swap(whole, "za", "zb")
    square = [swap(whole, a, b) for a, b in (("xa", "xb"), ("ya", "yb"), ("xaya", "xbyb"))]
    (both,) = join(((0, 1),), whole, near)
    back = swap(both, "zb", "za")
    (c0,) = join(((0, 1, 2, 3),), whole, *square)
    far, ahead = shift(back, 1), swap(back, "za", "zb")
    c3, c1, c2 = (swap(c0, b, a) for a, b in (("xaya", "xbyb"), ("xa", "xb"), ("ya", "yb")))
    e0 = swap_cores(c0)
    (p_far,) = pair([far], [c0, c1], F32)
    c1, c2, c3, ahead, p_far = lax.optimization_barrier((c1, c2, c3, ahead, p_far))
    e1, e2, e3 = swap_cores(c1), swap_cores(c2), swap_cores(c3)
    cols = [c0, c1, c2, c3, e0, e1, e2, e3]
    (p_far,) = pair([far], [c2, c3, e0, e1], F32, [p_far])
    (p_far,) = pair([far], [e2, e3], BF, [p_far])
    q = swap(p_far, "zb", "za")
    p_ahead, p_own = pair([ahead, both], cols, F32)
    q_near = swap(p_own[CPD:].astype(BF), "za", "zb")
    q = swap((p_ahead + q).astype(BF), "za", "zb")
    (p_back,) = pair([back], cols, F32)
    p_back = (p_back + q).astype(BF)
    arrived = (q_near, swap(p_back[:CPD], "zb", "za"), shift(p_back[CPD:], -1))

    rate = D * math.sqrt(D) / (3.0 * math.sqrt(classes))
    return pl.pallas_call(
        functools.partial(final_kernel, rate),
        out_shape=jax.ShapeDtypeStruct((CPD, D), F32),
        in_specs=[VMEM] * 5,
        out_specs=VMEM,
        compiler_params=pltpu.CompilerParams(vmem_limit_bytes=SMALL),
        name="final",
    )(embeddings, p_own[:CPD], *arrived)


def solution(mesh):
    in_specs = (P(("row", "col"), None), P(("row", "col")), P(("row", "col")))
    out_specs = P(("row", "col"), None)
    return jax.shard_map(per_device, mesh=mesh, in_specs=in_specs, out_specs=out_specs, check_vma=False)
```

```python
import functools
import itertools
import math

import jax
import jax.numpy as jnp
from jax import lax
from jax.experimental import pallas as pl
from jax.experimental.pallas import tpu as pltpu
from jax.sharding import PartitionSpec as P

BF = jnp.bfloat16
F32 = jnp.float32
D = 512
CPD = 128
META = 16
LANES = 128
CHUNKS = D // LANES
PACKED = CHUNKS * CPD + META
SMALL = 6 << 20
AXES = ("row", "col")
VMEM = pl.BlockSpec(memory_space=pltpu.VMEM)
ANY = pl.BlockSpec(memory_space=pl.ANY)


def _flat(x, y, z, core):
    return ((((z // 2) * 4 + x) * 2 + z % 2) * 4 + y) * 2 + core


LINKS = {
    "xa": lambda x, y, z: (x ^ 1, y, z),
    "xb": lambda x, y, z: (3 - x, y, z),
    "xaya": lambda x, y, z: (x ^ 1, y ^ 1, z),
    "xbyb": lambda x, y, z: (3 - x, 3 - y, z),
    "ya": lambda x, y, z: (x, y ^ 1, z),
    "yb": lambda x, y, z: (x, 3 - y, z),
    "za": lambda x, y, z: (x, y, z ^ 1),
    "zb": lambda x, y, z: (x, y, (z - 1) % 8 if z % 2 == 0 else (z + 1) % 8),
}


def swap(block, link0, link1):
    pairs = []
    for x, y, z, core in itertools.product(range(4), range(4), range(8), range(2)):
        pairs.append((_flat(x, y, z, core), _flat(*LINKS[(link0, link1)[core]](x, y, z), core)))
    return lax.ppermute(block, AXES, pairs)


def shift(block, sign):
    pairs = []
    for x, y, z, core in itertools.product(range(4), range(4), range(8), range(2)):
        step = 2 * sign * (1 if (z + core) % 2 == 0 else -1)
        pairs.append((_flat(x, y, z, core), _flat(x, y, (z + step) % 8, core)))
    return lax.ppermute(block, AXES, pairs)


def swap_cores(block):
    return lax.ppermute(block, AXES, [(i, i ^ 1) for i in range(256)])


def pack_kernel(emb_hbm, margin_hbm, group_hbm, whole, emb, margin, group, sem):
    pairs = ((emb_hbm, emb), (margin_hbm, margin), (group_hbm, group))
    copies = [pltpu.make_async_copy(src, dst, sem.at[i]) for i, (src, dst) in enumerate(pairs)]
    for c in copies:
        c.start()
    for c in copies:
        c.wait()
    e = emb[...]
    unit = (e / jnp.sqrt(jnp.sum(e * e, axis=1, keepdims=True) + 1e-06)).astype(BF)
    row = lax.broadcasted_iota(jnp.int32, (META, LANES), 0)
    meta = jnp.where(row == 0, margin[...], jnp.where(row == 1, group[...], 0)).astype(F32).astype(BF)
    for f in range(CHUNKS):
        whole[f * CPD : (f + 1) * CPD, :] = unit[:, f * LANES : (f + 1) * LANES]
    whole[CHUNKS * CPD :, :] = meta


def pack(embeddings, margin, group):
    return pl.pallas_call(
        pack_kernel,
        out_shape=jax.ShapeDtypeStruct((PACKED, LANES), BF),
        in_specs=[pl.BlockSpec(memory_space=pltpu.HBM)] * 3,
        out_specs=VMEM,
        scratch_shapes=[
            pltpu.VMEM((CPD, D), F32),
            pltpu.VMEM((1, CPD), jnp.int32),
            pltpu.VMEM((1, CPD), jnp.int32),
            pltpu.SemaphoreType.DMA((3,)),
        ],
        compiler_params=pltpu.CompilerParams(vmem_limit_bytes=SMALL),
        name="pack",
    )(embeddings, margin.reshape(1, CPD), group.reshape(1, CPD))


TB = 8


def units(ref, k):
    return jnp.concatenate([ref[k, f * CPD : (f + 1) * CPD, :] for f in range(CHUNKS)], axis=1)


def pair_kernel(n_r, n_c, n_sum, *refs):
    r_in, c_in, rest = refs[:n_r], refs[n_r : n_r + n_c], refs[n_r + n_c :]
    sums, outs = rest[:n_sum], rest[n_sum:]
    r_blocks, c_blocks = ([(ref, k) for ref in v for k in range(ref.shape[0])] for v in (r_in, c_in))
    acc, r_margin, r_group = [], [], []
    for i in range(0, len(r_blocks), 2):
        meta = [ref[k, CHUNKS * CPD :, :].astype(F32) for ref, k in r_blocks[i : i + 2]]
        r_margin.append(jnp.concatenate([jnp.broadcast_to(m[0:1] * 0.0005, (CPD, CPD)).T for m in meta], axis=0))
        r_group.append(jnp.concatenate([jnp.broadcast_to(m[1:2], (CPD, CPD)).T for m in meta], axis=0))
        acc.append(None)
    halves = [(ref, o) for ref in sums for o in range(0, ref.shape[0], 2 * CPD)]
    for i, (ref, o) in enumerate(halves):
        acc[i] = ref[o : o + 2 * CPD, :]
    for t in range(0, len(c_blocks), TB):
        tile = c_blocks[t : t + TB]
        meta = [ref[k, CHUNKS * CPD :, :].astype(F32) for ref, k in tile]
        ct = jnp.concatenate([units(ref, k) for ref, k in tile], axis=0)
        for i in range(len(acc)):
            rt = jnp.concatenate([units(ref, k) for ref, k in r_blocks[2 * i : 2 * i + 2]], axis=0)
            cos = lax.dot_general(rt, ct, (((1,), (1,)), ((), ())), preferred_element_type=F32)
            parts = []
            for k, m in enumerate(meta):
                over = jnp.maximum(cos[:, k * LANES : (k + 1) * LANES] - r_margin[i] - m[0:1] * 0.0005, 0.0)
                parts.append(jnp.where(r_group[i] != m[1:2], over, 0.0).astype(BF))
            part = jnp.dot(jnp.concatenate(parts, axis=1), ct, preferred_element_type=F32)
            acc[i] = part if acc[i] is None else acc[i] + part
    halves = [(ref, o) for ref in outs for o in range(0, ref.shape[0], 2 * CPD)]
    for i, (ref, o) in enumerate(halves):
        ref[o : o + 2 * CPD, :] = acc[i].astype(ref.dtype)


def pair(r_in, c_in, out_dtype, sums=()):
    r_in, c_in = ([a.reshape(-1, PACKED, LANES) for a in v] for v in (r_in, c_in))
    rows, cols = (sum(a.shape[0] for a in v) * CPD for v in (r_in, c_in))
    return pl.pallas_call(
        functools.partial(pair_kernel, len(r_in), len(c_in), len(sums)),
        out_shape=[jax.ShapeDtypeStruct((a.shape[0] * CPD, D), out_dtype) for a in r_in],
        in_specs=[VMEM] * (len(r_in) + len(c_in) + len(sums)),
        out_specs=[VMEM] * len(r_in),
        compiler_params=pltpu.CompilerParams(vmem_limit_bytes=20 << 20),
        cost_estimate=pl.CostEstimate(
            flops=4 * rows * cols * D, bytes_accessed=(cols + rows) * D * 2, transcendentals=0
        ),
        name="pair",
    )(*r_in, *c_in, *sums)


def join_kernel(pieces, n_in, *refs):
    ins, outs, sem = refs[:n_in], refs[n_in:-1], refs[-1]
    copies = []
    for out, which in zip(outs, pieces, strict=True):
        at = 0
        for i in which:
            n = ins[i].shape[0]
            copies.append(pltpu.make_async_copy(ins[i], out.at[at : at + n], sem.at[len(copies)]))
            at += n
    for c in copies:
        c.start()
    for c in copies:
        c.wait()


def join(pieces, *ins):
    return pl.pallas_call(
        functools.partial(join_kernel, pieces, len(ins)),
        out_shape=[jax.ShapeDtypeStruct((sum(ins[i].shape[0] for i in p), LANES), BF) for p in pieces],
        in_specs=[ANY] * len(ins),
        out_specs=[VMEM] * len(pieces),
        scratch_shapes=[pltpu.SemaphoreType.DMA((sum(map(len, pieces)),))],
        compiler_params=pltpu.CompilerParams(vmem_limit_bytes=SMALL),
        name="join",
    )(*ins)


def final_kernel(rate, emb, own, *refs):
    arrived, out = refs[:-1], refs[-1]
    e = emb[...]
    lengths = jnp.sqrt(jnp.sum(e * e, axis=1, keepdims=True) + 1e-06)
    unit = e / lengths
    grad = 4.0 * sum((ref[...].astype(F32) for ref in arrived), own[...])
    radial = jnp.sum(unit * grad, axis=1, keepdims=True)
    out[...] = e - rate * ((grad - unit * radial) / lengths)


def per_device(embeddings, margin, group):
    classes = embeddings.shape[0] * lax.axis_size("row") * lax.axis_size("col")
    whole = pack(embeddings, margin, group)

    near = swap(whole, "za", "zb")
    square = [swap(whole, a, b) for a, b in (("xaya", "xbyb"), ("xa", "xb"), ("ya", "yb"))]
    (both,) = join(((0, 1),), whole, near)
    back = swap(both, "zb", "za")
    (c0,) = join(((3, 0, 1, 2),), *square, whole)
    far, ahead = shift(back, 1), swap(back, "za", "zb")
    c3, c1, c2 = (swap(c0, b, a) for a, b in (("xaya", "xbyb"), ("xa", "xb"), ("ya", "yb")))
    e0 = swap_cores(c0)
    (p_far,) = pair([far], [c0, c1], F32)
    c2, c3, ahead, p_far = lax.optimization_barrier((c2, c3, ahead, p_far))
    e1, e2, e3 = swap_cores(c1), swap_cores(c2), swap_cores(c3)
    cols = [c0, c1, c2, c3, e0, e1, e2, e3]
    (p_far,) = pair([far], [c2, c3, e0, e1], F32, [p_far])
    (p_far,) = pair([far], [e2, e3], BF, [p_far])
    q = swap(p_far, "zb", "za")
    p_ahead, p_own = pair([ahead, both], cols, F32)
    q_near = swap(p_own[CPD:].astype(BF), "za", "zb")
    q = swap((p_ahead + q).astype(BF), "za", "zb")
    (p_back,) = pair([back], cols, F32)
    p_back = (p_back + q).astype(BF)
    arrived = (q_near, shift(p_back[CPD:], -1), swap(p_back[:CPD], "zb", "za"))

    rate = D * math.sqrt(D) / (3.0 * math.sqrt(classes))
    return pl.pallas_call(
        functools.partial(final_kernel, rate),
        out_shape=jax.ShapeDtypeStruct((CPD, D), F32),
        in_specs=[VMEM] * 5,
        out_specs=VMEM,
        compiler_params=pltpu.CompilerParams(vmem_limit_bytes=SMALL),
        name="final",
    )(embeddings, p_own[:CPD], *arrived)


def solution(mesh):
    in_specs = (P(("row", "col"), None), P(("row", "col")), P(("row", "col")))
    out_specs = P(("row", "col"), None)
    return jax.shard_map(per_device, mesh=mesh, in_specs=in_specs, out_specs=out_specs, check_vma=False)
```

```python
import functools
import itertools
import math

import jax
import jax.numpy as jnp
from jax import lax
from jax.experimental import pallas as pl
from jax.experimental.pallas import tpu as pltpu
from jax.sharding import PartitionSpec as P

BF = jnp.bfloat16
F32 = jnp.float32
D = 512
CPD = 128
META = 16
LANES = 128
CHUNKS = D // LANES
PACKED = CHUNKS * CPD + META
SMALL = 6 << 20
AXES = ("row", "col")
VMEM = pl.BlockSpec(memory_space=pltpu.VMEM)


def _flat(x, y, z, core):
    return ((((z // 2) * 4 + x) * 2 + z % 2) * 4 + y) * 2 + core


LINKS = {
    "xa": lambda x, y, z: (x ^ 1, y, z),
    "xb": lambda x, y, z: (3 - x, y, z),
    "xaya": lambda x, y, z: (x ^ 1, y ^ 1, z),
    "xbyb": lambda x, y, z: (3 - x, 3 - y, z),
    "ya": lambda x, y, z: (x, y ^ 1, z),
    "yb": lambda x, y, z: (x, 3 - y, z),
    "za": lambda x, y, z: (x, y, z ^ 1),
    "zb": lambda x, y, z: (x, y, (z - 1) % 8 if z % 2 == 0 else (z + 1) % 8),
}


def swap(block, link0, link1):
    pairs = []
    for x, y, z, core in itertools.product(range(4), range(4), range(8), range(2)):
        pairs.append((_flat(x, y, z, core), _flat(*LINKS[(link0, link1)[core]](x, y, z), core)))
    return lax.ppermute(block, AXES, pairs)


def shift(block, sign):
    pairs = []
    for x, y, z, core in itertools.product(range(4), range(4), range(8), range(2)):
        step = 2 * sign * (1 if (z + core) % 2 == 0 else -1)
        pairs.append((_flat(x, y, z, core), _flat(x, y, (z + step) % 8, core)))
    return lax.ppermute(block, AXES, pairs)


def swap_cores(block):
    return lax.ppermute(block, AXES, [(i, i ^ 1) for i in range(256)])


def units_kernel(emb, out):
    e = emb[...]
    unit = (e / jnp.sqrt(jnp.sum(e * e, axis=1, keepdims=True) + 1e-06)).astype(BF)
    for f in range(CHUNKS):
        out[f * CPD : (f + 1) * CPD, :] = unit[:, f * LANES : (f + 1) * LANES]


def pack_kernel(unit, margin, group, whole):
    row = lax.broadcasted_iota(jnp.int32, (META, LANES), 0)
    meta = jnp.where(row == 0, margin[...], jnp.where(row == 1, group[...], 0)).astype(F32).astype(BF)
    whole[: CHUNKS * CPD, :] = unit[...]
    whole[CHUNKS * CPD :, :] = meta


def pack(embeddings, margin, group):
    params = pltpu.CompilerParams(vmem_limit_bytes=SMALL)
    unit = pl.pallas_call(
        units_kernel,
        out_shape=jax.ShapeDtypeStruct((CHUNKS * CPD, LANES), BF),
        in_specs=[VMEM],
        out_specs=VMEM,
        compiler_params=params,
        name="units",
    )(embeddings)
    return pl.pallas_call(
        pack_kernel,
        out_shape=jax.ShapeDtypeStruct((PACKED, LANES), BF),
        in_specs=[VMEM] * 3,
        out_specs=VMEM,
        compiler_params=params,
        name="pack",
    )(unit, margin.reshape(1, CPD), group.reshape(1, CPD))


TB = 8


def units(ref, k):
    return jnp.concatenate([ref[k, f * CPD : (f + 1) * CPD, :] for f in range(CHUNKS)], axis=1)


def pair_kernel(n_r, n_c, n_sum, *refs):
    r_in, c_in, rest = refs[:n_r], refs[n_r : n_r + n_c], refs[n_r + n_c :]
    sums, outs = rest[:n_sum], rest[n_sum:]
    r_blocks, c_blocks = ([(ref, k) for ref in v for k in range(ref.shape[0])] for v in (r_in, c_in))
    acc, r_margin, r_group = [], [], []
    for i in range(0, len(r_blocks), 2):
        meta = [ref[k, CHUNKS * CPD :, :].astype(F32) for ref, k in r_blocks[i : i + 2]]
        r_margin.append(jnp.concatenate([jnp.broadcast_to(m[0:1] * 0.0005, (CPD, CPD)).T for m in meta], axis=0))
        r_group.append(jnp.concatenate([jnp.broadcast_to(m[1:2], (CPD, CPD)).T for m in meta], axis=0))
        acc.append(None)
    halves = [(ref, o) for ref in sums for o in range(0, ref.shape[0], 2 * CPD)]
    for i, (ref, o) in enumerate(halves):
        acc[i] = ref[o : o + 2 * CPD, :]
    for t in range(0, len(c_blocks), TB):
        tile = c_blocks[t : t + TB]
        meta = [ref[k, CHUNKS * CPD :, :].astype(F32) for ref, k in tile]
        ct = jnp.concatenate([units(ref, k) for ref, k in tile], axis=0)
        for i in range(len(acc)):
            rt = jnp.concatenate([units(ref, k) for ref, k in r_blocks[2 * i : 2 * i + 2]], axis=0)
            cos = lax.dot_general(rt, ct, (((1,), (1,)), ((), ())), preferred_element_type=F32)
            parts = []
            for k, m in enumerate(meta):
                over = jnp.maximum(cos[:, k * LANES : (k + 1) * LANES] - r_margin[i] - m[0:1] * 0.0005, 0.0)
                parts.append(jnp.where(r_group[i] != m[1:2], over, 0.0).astype(BF))
            part = jnp.dot(jnp.concatenate(parts, axis=1), ct, preferred_element_type=F32)
            acc[i] = part if acc[i] is None else acc[i] + part
    halves = [(ref, o) for ref in outs for o in range(0, ref.shape[0], 2 * CPD)]
    for i, (ref, o) in enumerate(halves):
        ref[o : o + 2 * CPD, :] = acc[i].astype(ref.dtype)


def pair(r_in, c_in, out_dtype, sums=()):
    r_in, c_in = ([a.reshape(-1, PACKED, LANES) for a in v] for v in (r_in, c_in))
    rows, cols = (sum(a.shape[0] for a in v) * CPD for v in (r_in, c_in))
    return pl.pallas_call(
        functools.partial(pair_kernel, len(r_in), len(c_in), len(sums)),
        out_shape=[jax.ShapeDtypeStruct((a.shape[0] * CPD, D), out_dtype) for a in r_in],
        in_specs=[VMEM] * (len(r_in) + len(c_in) + len(sums)),
        out_specs=[VMEM] * len(r_in),
        compiler_params=pltpu.CompilerParams(vmem_limit_bytes=20 << 20),
        cost_estimate=pl.CostEstimate(
            flops=4 * rows * cols * D, bytes_accessed=(cols + rows) * D * 2, transcendentals=0
        ),
        name="pair",
    )(*r_in, *c_in, *sums)


def join_kernel(*refs):
    ins, out = refs[:-1], refs[-1]
    at = 0
    for ref in ins:
        n = ref.shape[0]
        out[at : at + n, :] = ref[...]
        at += n


def join(*ins):
    return pl.pallas_call(
        join_kernel,
        out_shape=jax.ShapeDtypeStruct((sum(a.shape[0] for a in ins), LANES), BF),
        in_specs=[VMEM] * len(ins),
        out_specs=VMEM,
        compiler_params=pltpu.CompilerParams(vmem_limit_bytes=SMALL),
        name="join",
    )(*ins)


def final_kernel(rate, emb, own, *refs):
    arrived, out = refs[:-1], refs[-1]
    e = emb[...]
    lengths = jnp.sqrt(jnp.sum(e * e, axis=1, keepdims=True) + 1e-06)
    unit = e / lengths
    grad = 4.0 * sum((ref[...].astype(F32) for ref in arrived), own[...])
    radial = jnp.sum(unit * grad, axis=1, keepdims=True)
    out[...] = e - rate * ((grad - unit * radial) / lengths)


def per_device(embeddings, margin, group):
    classes = embeddings.shape[0] * lax.axis_size("row") * lax.axis_size("col")
    whole = pack(embeddings, margin, group)

    near = swap(whole, "za", "zb")
    square = [swap(whole, a, b) for a, b in (("xaya", "xbyb"), ("xa", "xb"), ("ya", "yb"))]
    both = join(whole, near)
    back = swap(both, "zb", "za")
    c0 = join(*square, whole)
    far, ahead = shift(back, 1), swap(back, "za", "zb")
    c3, c1, c2 = (swap(c0, b, a) for a, b in (("xaya", "xbyb"), ("xa", "xb"), ("ya", "yb")))
    e0 = swap_cores(c0)
    (p_far,) = pair([far], [c0, c1], F32)
    c2, c3, ahead, p_far = lax.optimization_barrier((c2, c3, ahead, p_far))
    e1, e2, e3 = swap_cores(c1), swap_cores(c2), swap_cores(c3)
    cols = [c0, c1, c2, c3, e0, e1, e2, e3]
    (p_far,) = pair([far], [c2, c3, e0, e1], F32, [p_far])
    (p_far,) = pair([far], [e2, e3], BF, [p_far])
    q = swap(p_far, "zb", "za")
    p_ahead, p_own = pair([ahead, both], cols, F32)
    q_near = swap(p_own[CPD:].astype(BF), "za", "zb")
    q = swap((p_ahead + q).astype(BF), "za", "zb")
    (p_back,) = pair([back], cols, F32)
    p_back = (p_back + q).astype(BF)
    arrived = (q_near, shift(p_back[CPD:], -1), swap(p_back[:CPD], "zb", "za"))

    rate = D * math.sqrt(D) / (3.0 * math.sqrt(classes))
    return pl.pallas_call(
        functools.partial(final_kernel, rate),
        out_shape=jax.ShapeDtypeStruct((CPD, D), F32),
        in_specs=[VMEM] * 5,
        out_specs=VMEM,
        compiler_params=pltpu.CompilerParams(vmem_limit_bytes=SMALL),
        name="final",
    )(embeddings, p_own[:CPD], *arrived)


def solution(mesh):
    in_specs = (P(("row", "col"), None), P(("row", "col")), P(("row", "col")))
    out_specs = P(("row", "col"), None)
    return jax.shard_map(per_device, mesh=mesh, in_specs=in_specs, out_specs=out_specs, check_vma=False)
```

```python
import functools
import itertools
import math

import jax
import jax.numpy as jnp
from jax import lax
from jax.experimental import pallas as pl
from jax.experimental.pallas import tpu as pltpu
from jax.sharding import PartitionSpec as P

BF = jnp.bfloat16
F32 = jnp.float32
D = 512
CPD = 128
META = 16
LANES = 128
CHUNKS = D // LANES
UNITS = CHUNKS * CPD
SMALL = 6 << 20
AXES = ("row", "col")
VMEM = pl.BlockSpec(memory_space=pltpu.VMEM)


def _flat(x, y, z, core):
    return ((((z // 2) * 4 + x) * 2 + z % 2) * 4 + y) * 2 + core


LINKS = {
    "xa": lambda x, y, z: (x ^ 1, y, z),
    "xb": lambda x, y, z: (3 - x, y, z),
    "xaya": lambda x, y, z: (x ^ 1, y ^ 1, z),
    "xbyb": lambda x, y, z: (3 - x, 3 - y, z),
    "ya": lambda x, y, z: (x, y ^ 1, z),
    "yb": lambda x, y, z: (x, 3 - y, z),
    "za": lambda x, y, z: (x, y, z ^ 1),
    "zb": lambda x, y, z: (x, y, (z - 1) % 8 if z % 2 == 0 else (z + 1) % 8),
}


def swap(block, link0, link1):
    pairs = []
    for x, y, z, core in itertools.product(range(4), range(4), range(8), range(2)):
        pairs.append((_flat(x, y, z, core), _flat(*LINKS[(link0, link1)[core]](x, y, z), core)))
    return lax.ppermute(block, AXES, pairs)


def shift(block, sign):
    pairs = []
    for x, y, z, core in itertools.product(range(4), range(4), range(8), range(2)):
        step = 2 * sign * (1 if (z + core) % 2 == 0 else -1)
        pairs.append((_flat(x, y, z, core), _flat(x, y, (z + step) % 8, core)))
    return lax.ppermute(block, AXES, pairs)


def swap_cores(block):
    return lax.ppermute(block, AXES, [(i, i ^ 1) for i in range(256)])


def units_kernel(emb, out):
    e = emb[...]
    unit = (e / jnp.sqrt(jnp.sum(e * e, axis=1, keepdims=True) + 1e-06)).astype(BF)
    for f in range(CHUNKS):
        out[f * CPD : (f + 1) * CPD, :] = unit[:, f * LANES : (f + 1) * LANES]


def pack_kernel(unit, margin, group, whole):
    row = lax.broadcasted_iota(jnp.int32, (META, LANES), 0)
    meta = jnp.where(row == 0, margin[...], jnp.where(row == 1, group[...], 0)).astype(F32).astype(BF)
    whole[:UNITS, :] = unit[...]
    whole[UNITS:, :] = meta


def pack(embeddings, margin, group):
    params = pltpu.CompilerParams(vmem_limit_bytes=SMALL)
    unit = pl.pallas_call(
        units_kernel,
        out_shape=jax.ShapeDtypeStruct((UNITS, LANES), BF),
        in_specs=[VMEM],
        out_specs=VMEM,
        compiler_params=params,
        name="units",
    )(embeddings)
    return pl.pallas_call(
        pack_kernel,
        out_shape=jax.ShapeDtypeStruct((UNITS + META, LANES), BF),
        in_specs=[VMEM] * 3,
        out_specs=VMEM,
        compiler_params=params,
        name="pack",
    )(unit, margin.reshape(1, CPD), group.reshape(1, CPD))


TB = 8


def units(ref, k):
    at = k * UNITS
    return jnp.concatenate([ref[at + f * CPD : at + (f + 1) * CPD, :] for f in range(CHUNKS)], axis=1)


def marks(ref, k):
    meta = ref[ref.shape[0] - META :, :].astype(F32)
    return meta[2 * k : 2 * k + 1], meta[2 * k + 1 : 2 * k + 2]


def blocks(ref):
    return (ref.shape[0] - META) // UNITS


def pair_kernel(n_r, n_c, n_sum, *refs):
    r_in, c_in, rest = refs[:n_r], refs[n_r : n_r + n_c], refs[n_r + n_c :]
    sums, outs = rest[:n_sum], rest[n_sum:]
    r_blocks, c_blocks = ([(ref, k) for ref in v for k in range(blocks(ref))] for v in (r_in, c_in))
    acc, r_margin, r_group = [], [], []
    for i in range(0, len(r_blocks), 2):
        meta = [marks(ref, k) for ref, k in r_blocks[i : i + 2]]
        r_margin.append(jnp.concatenate([jnp.broadcast_to(m * 0.0005, (CPD, CPD)).T for m, _ in meta], axis=0))
        r_group.append(jnp.concatenate([jnp.broadcast_to(g, (CPD, CPD)).T for _, g in meta], axis=0))
        acc.append(None)
    halves = [(ref, o) for ref in sums for o in range(0, ref.shape[0], 2 * CPD)]
    for i, (ref, o) in enumerate(halves):
        acc[i] = ref[o : o + 2 * CPD, :]
    for t in range(0, len(c_blocks), TB):
        tile = c_blocks[t : t + TB]
        meta = [marks(ref, k) for ref, k in tile]
        ct = jnp.concatenate([units(ref, k) for ref, k in tile], axis=0)
        for i in range(len(acc)):
            rt = jnp.concatenate([units(ref, k) for ref, k in r_blocks[2 * i : 2 * i + 2]], axis=0)
            cos = lax.dot_general(rt, ct, (((1,), (1,)), ((), ())), preferred_element_type=F32)
            parts = []
            for k, (m, g) in enumerate(meta):
                over = jnp.maximum(cos[:, k * LANES : (k + 1) * LANES] - r_margin[i] - m * 0.0005, 0.0)
                parts.append(jnp.where(r_group[i] != g, over, 0.0).astype(BF))
            part = jnp.dot(jnp.concatenate(parts, axis=1), ct, preferred_element_type=F32)
            acc[i] = part if acc[i] is None else acc[i] + part
    halves = [(ref, o) for ref in outs for o in range(0, ref.shape[0], 2 * CPD)]
    for i, (ref, o) in enumerate(halves):
        ref[o : o + 2 * CPD, :] = acc[i].astype(ref.dtype)


def pair(r_in, c_in, out_dtype, sums=()):
    rows, cols = (sum(blocks(a) for a in v) * CPD for v in (r_in, c_in))
    return pl.pallas_call(
        functools.partial(pair_kernel, len(r_in), len(c_in), len(sums)),
        out_shape=[jax.ShapeDtypeStruct((blocks(a) * CPD, D), out_dtype) for a in r_in],
        in_specs=[VMEM] * (len(r_in) + len(c_in) + len(sums)),
        out_specs=[VMEM] * len(r_in),
        compiler_params=pltpu.CompilerParams(vmem_limit_bytes=20 << 20),
        cost_estimate=pl.CostEstimate(
            flops=4 * rows * cols * D, bytes_accessed=(cols + rows) * D * 2, transcendentals=0
        ),
        name="pair",
    )(*r_in, *c_in, *sums)


def join_kernel(*refs):
    ins, out = refs[:-1], refs[-1]
    row = lax.broadcasted_iota(jnp.int32, (META, LANES), 0)
    meta = jnp.zeros((META, LANES), F32)
    for i, ref in enumerate(ins):
        out[i * UNITS : (i + 1) * UNITS, :] = ref[:UNITS, :]
        margin, group = marks(ref, 0)
        meta = jnp.where(row == 2 * i, margin, jnp.where(row == 2 * i + 1, group, meta))
    out[len(ins) * UNITS :, :] = meta.astype(BF)


def join(*ins):
    return pl.pallas_call(
        join_kernel,
        out_shape=jax.ShapeDtypeStruct((len(ins) * UNITS + META, LANES), BF),
        in_specs=[VMEM] * len(ins),
        out_specs=VMEM,
        compiler_params=pltpu.CompilerParams(vmem_limit_bytes=SMALL),
        name="join",
    )(*ins)


def final_kernel(rate, emb, own, *refs):
    arrived, out = refs[:-1], refs[-1]
    e = emb[...]
    lengths = jnp.sqrt(jnp.sum(e * e, axis=1, keepdims=True) + 1e-06)
    unit = e / lengths
    grad = 4.0 * sum((ref[...].astype(F32) for ref in arrived), own[...])
    radial = jnp.sum(unit * grad, axis=1, keepdims=True)
    out[...] = e - rate * ((grad - unit * radial) / lengths)


def per_device(embeddings, margin, group):
    classes = embeddings.shape[0] * lax.axis_size("row") * lax.axis_size("col")
    whole = pack(embeddings, margin, group)

    near = swap(whole, "za", "zb")
    square = [swap(whole, a, b) for a, b in (("xaya", "xbyb"), ("xa", "xb"), ("ya", "yb"))]
    both = join(whole, near)
    back = swap(both, "zb", "za")
    c0 = join(*square, whole)
    far, ahead = shift(back, 1), swap(back, "za", "zb")
    c3, c1, c2 = (swap(c0, b, a) for a, b in (("xaya", "xbyb"), ("xa", "xb"), ("ya", "yb")))
    e0 = swap_cores(c0)
    (p_far,) = pair([far], [c0, c1], F32)
    c2, c3, ahead, p_far = lax.optimization_barrier((c2, c3, ahead, p_far))
    e1, e2, e3 = swap_cores(c1), swap_cores(c2), swap_cores(c3)
    cols = [c0, c1, c2, c3, e0, e1, e2, e3]
    (p_far,) = pair([far], [c2, c3, e0, e1], F32, [p_far])
    (p_far,) = pair([far], [e2, e3], BF, [p_far])
    q = swap(p_far, "zb", "za")
    p_ahead, p_back = pair([ahead, back], cols, F32)
    q = swap((p_ahead + q).astype(BF), "za", "zb")
    (p_own,) = pair([both], cols, F32)
    q_near = swap(p_own[CPD:].astype(BF), "za", "zb")
    p_back = (p_back + q).astype(BF)
    arrived = (q_near, shift(p_back[CPD:], -1), swap(p_back[:CPD], "zb", "za"))

    rate = D * math.sqrt(D) / (3.0 * math.sqrt(classes))
    return pl.pallas_call(
        functools.partial(final_kernel, rate),
        out_shape=jax.ShapeDtypeStruct((CPD, D), F32),
        in_specs=[VMEM] * 5,
        out_specs=VMEM,
        compiler_params=pltpu.CompilerParams(vmem_limit_bytes=SMALL),
        name="final",
    )(embeddings, p_own[:CPD], *arrived)


def solution(mesh):
    in_specs = (P(("row", "col"), None), P(("row", "col")), P(("row", "col")))
    out_specs = P(("row", "col"), None)
    return jax.shard_map(per_device, mesh=mesh, in_specs=in_specs, out_specs=out_specs, check_vma=False)
```

```python
import functools
import itertools
import math

import jax
import jax.numpy as jnp
from jax import lax
from jax.experimental import pallas as pl
from jax.experimental.pallas import tpu as pltpu
from jax.sharding import PartitionSpec as P

BF = jnp.bfloat16
F32 = jnp.float32
D = 512
CPD = 128
META = 16
LANES = 128
CHUNKS = D // LANES
UNITS = CHUNKS * CPD
SMALL = 6 << 20
AXES = ("row", "col")
VMEM = pl.BlockSpec(memory_space=pltpu.VMEM)


def _flat(x, y, z, core):
    return ((((z // 2) * 4 + x) * 2 + z % 2) * 4 + y) * 2 + core


LINKS = {
    "xa": lambda x, y, z: (x ^ 1, y, z),
    "xb": lambda x, y, z: (3 - x, y, z),
    "xayb": lambda x, y, z: (x ^ 1, 3 - y, z),
    "xbya": lambda x, y, z: (3 - x, y ^ 1, z),
    "ya": lambda x, y, z: (x, y ^ 1, z),
    "yb": lambda x, y, z: (x, 3 - y, z),
    "za": lambda x, y, z: (x, y, z ^ 1),
    "zb": lambda x, y, z: (x, y, (z - 1) % 8 if z % 2 == 0 else (z + 1) % 8),
}


def swap(block, link0, link1):
    pairs = []
    for x, y, z, core in itertools.product(range(4), range(4), range(8), range(2)):
        pairs.append((_flat(x, y, z, core), _flat(*LINKS[(link0, link1)[core]](x, y, z), core)))
    return lax.ppermute(block, AXES, pairs)


def shift(block, sign):
    pairs = []
    for x, y, z, core in itertools.product(range(4), range(4), range(8), range(2)):
        step = 2 * sign * (1 if (z + core) % 2 == 0 else -1)
        pairs.append((_flat(x, y, z, core), _flat(x, y, (z + step) % 8, core)))
    return lax.ppermute(block, AXES, pairs)


def swap_cores(block):
    return lax.ppermute(block, AXES, [(i, i ^ 1) for i in range(256)])


def units_kernel(emb, out):
    e = emb[...]
    unit = (e / jnp.sqrt(jnp.sum(e * e, axis=1, keepdims=True) + 1e-06)).astype(BF)
    for f in range(CHUNKS):
        out[f * CPD : (f + 1) * CPD, :] = unit[:, f * LANES : (f + 1) * LANES]


def pack_kernel(unit, margin, group, whole):
    row = lax.broadcasted_iota(jnp.int32, (META, LANES), 0)
    meta = jnp.where(row == 0, margin[...], jnp.where(row == 1, group[...], 0)).astype(F32).astype(BF)
    whole[:UNITS, :] = unit[...]
    whole[UNITS:, :] = meta


def pack(embeddings, margin, group):
    params = pltpu.CompilerParams(vmem_limit_bytes=SMALL)
    unit = pl.pallas_call(
        units_kernel,
        out_shape=jax.ShapeDtypeStruct((UNITS, LANES), BF),
        in_specs=[VMEM],
        out_specs=VMEM,
        compiler_params=params,
        name="units",
    )(embeddings)
    return pl.pallas_call(
        pack_kernel,
        out_shape=jax.ShapeDtypeStruct((UNITS + META, LANES), BF),
        in_specs=[VMEM] * 3,
        out_specs=VMEM,
        compiler_params=params,
        name="pack",
    )(unit, margin.reshape(1, CPD), group.reshape(1, CPD))


TB = 8


def units(ref, k):
    at = k * UNITS
    return jnp.concatenate([ref[at + f * CPD : at + (f + 1) * CPD, :] for f in range(CHUNKS)], axis=1)


def marks(ref, k):
    meta = ref[ref.shape[0] - META :, :].astype(F32)
    return meta[2 * k : 2 * k + 1], meta[2 * k + 1 : 2 * k + 2]


def blocks(ref):
    return (ref.shape[0] - META) // UNITS


def pair_kernel(n_r, n_c, n_sum, *refs):
    r_in, c_in, rest = refs[:n_r], refs[n_r : n_r + n_c], refs[n_r + n_c :]
    sums, outs = rest[:n_sum], rest[n_sum:]
    r_blocks, c_blocks = ([(ref, k) for ref in v for k in range(blocks(ref))] for v in (r_in, c_in))
    acc, r_margin, r_group = [], [], []
    for i in range(0, len(r_blocks), 2):
        meta = [marks(ref, k) for ref, k in r_blocks[i : i + 2]]
        r_margin.append(jnp.concatenate([jnp.broadcast_to(m * 0.0005, (CPD, CPD)).T for m, _ in meta], axis=0))
        r_group.append(jnp.concatenate([jnp.broadcast_to(g, (CPD, CPD)).T for _, g in meta], axis=0))
        acc.append(None)
    halves = [(ref, o) for ref in sums for o in range(0, ref.shape[0], 2 * CPD)]
    for i, (ref, o) in enumerate(halves):
        acc[i] = ref[o : o + 2 * CPD, :]
    for t in range(0, len(c_blocks), TB):
        tile = c_blocks[t : t + TB]
        meta = [marks(ref, k) for ref, k in tile]
        ct = jnp.concatenate([units(ref, k) for ref, k in tile], axis=0)
        for i in range(len(acc)):
            rt = jnp.concatenate([units(ref, k) for ref, k in r_blocks[2 * i : 2 * i + 2]], axis=0)
            cos = lax.dot_general(rt, ct, (((1,), (1,)), ((), ())), preferred_element_type=F32)
            parts = []
            for k, (m, g) in enumerate(meta):
                over = jnp.maximum(cos[:, k * LANES : (k + 1) * LANES] - r_margin[i] - m * 0.0005, 0.0)
                parts.append(jnp.where(r_group[i] != g, over, 0.0).astype(BF))
            part = jnp.dot(jnp.concatenate(parts, axis=1), ct, preferred_element_type=F32)
            acc[i] = part if acc[i] is None else acc[i] + part
    halves = [(ref, o) for ref in outs for o in range(0, ref.shape[0], 2 * CPD)]
    for i, (ref, o) in enumerate(halves):
        ref[o : o + 2 * CPD, :] = acc[i].astype(ref.dtype)


def pair(r_in, c_in, out_dtype, sums=()):
    rows, cols = (sum(blocks(a) for a in v) * CPD for v in (r_in, c_in))
    return pl.pallas_call(
        functools.partial(pair_kernel, len(r_in), len(c_in), len(sums)),
        out_shape=[jax.ShapeDtypeStruct((blocks(a) * CPD, D), out_dtype) for a in r_in],
        in_specs=[VMEM] * (len(r_in) + len(c_in) + len(sums)),
        out_specs=[VMEM] * len(r_in),
        compiler_params=pltpu.CompilerParams(vmem_limit_bytes=20 << 20),
        cost_estimate=pl.CostEstimate(
            flops=4 * rows * cols * D, bytes_accessed=(cols + rows) * D * 2, transcendentals=0
        ),
        name="pair",
    )(*r_in, *c_in, *sums)


def join_kernel(*refs):
    ins, out = refs[:-1], refs[-1]
    row = lax.broadcasted_iota(jnp.int32, (META, LANES), 0)
    meta = jnp.zeros((META, LANES), F32)
    for i, ref in enumerate(ins):
        out[i * UNITS : (i + 1) * UNITS, :] = ref[:UNITS, :]
        margin, group = marks(ref, 0)
        meta = jnp.where(row == 2 * i, margin, jnp.where(row == 2 * i + 1, group, meta))
    out[len(ins) * UNITS :, :] = meta.astype(BF)


def join(*ins):
    return pl.pallas_call(
        join_kernel,
        out_shape=jax.ShapeDtypeStruct((len(ins) * UNITS + META, LANES), BF),
        in_specs=[VMEM] * len(ins),
        out_specs=VMEM,
        compiler_params=pltpu.CompilerParams(vmem_limit_bytes=SMALL),
        name="join",
    )(*ins)


def final_kernel(rate, emb, own, *refs):
    arrived, out = refs[:-1], refs[-1]
    e = emb[...]
    lengths = jnp.sqrt(jnp.sum(e * e, axis=1, keepdims=True) + 1e-06)
    unit = e / lengths
    grad = 4.0 * sum((ref[...].astype(F32) for ref in arrived), own[...])
    radial = jnp.sum(unit * grad, axis=1, keepdims=True)
    out[...] = e - rate * ((grad - unit * radial) / lengths)


def per_device(embeddings, margin, group):
    classes = embeddings.shape[0] * lax.axis_size("row") * lax.axis_size("col")
    whole = pack(embeddings, margin, group)

    near = swap(whole, "za", "zb")
    square = [swap(whole, a, b) for a, b in (("xbya", "xayb"), ("xb", "xa"), ("ya", "yb"))]
    both = join(whole, near)
    back = swap(both, "zb", "za")
    c0 = join(*square, whole)
    far, ahead = shift(back, 1), swap(back, "za", "zb")
    c3, c1, c2 = (swap(c0, b, a) for a, b in (("xbya", "xayb"), ("xb", "xa"), ("ya", "yb")))
    e0 = swap_cores(c0)
    (p_far,) = pair([far], [c0, c1], F32)
    c2, c3, ahead, p_far = lax.optimization_barrier((c2, c3, ahead, p_far))
    e1, e2, e3 = swap_cores(c1), swap_cores(c2), swap_cores(c3)
    cols = [c0, c1, c2, c3, e0, e1, e2, e3]
    (p_far,) = pair([far], [c2, c3, e0, e1], F32, [p_far])
    (p_far,) = pair([far], [e2, e3], BF, [p_far])
    q = swap(p_far, "zb", "za")
    p_ahead, p_back = pair([ahead, back], cols, F32)
    q = swap((p_ahead + q).astype(BF), "za", "zb")
    (p_own,) = pair([both], cols, F32)
    q_near = swap(p_own[CPD:].astype(BF), "za", "zb")
    p_back = (p_back + q).astype(BF)
    arrived = (q_near, shift(p_back[CPD:], -1), swap(p_back[:CPD], "zb", "za"))

    rate = D * math.sqrt(D) / (3.0 * math.sqrt(classes))
    return pl.pallas_call(
        functools.partial(final_kernel, rate),
        out_shape=jax.ShapeDtypeStruct((CPD, D), F32),
        in_specs=[VMEM] * 5,
        out_specs=VMEM,
        compiler_params=pltpu.CompilerParams(vmem_limit_bytes=SMALL),
        name="final",
    )(embeddings, p_own[:CPD], *arrived)


def solution(mesh):
    in_specs = (P(("row", "col"), None), P(("row", "col")), P(("row", "col")))
    out_specs = P(("row", "col"), None)
    return jax.shard_map(per_device, mesh=mesh, in_specs=in_specs, out_specs=out_specs, check_vma=False)
```

```python
import functools
import itertools
import math

import jax
import jax.numpy as jnp
from jax import lax
from jax.experimental import pallas as pl
from jax.experimental.pallas import tpu as pltpu
from jax.sharding import PartitionSpec as P

BF = jnp.bfloat16
F32 = jnp.float32
D = 512
CPD = 128
META = 16
LANES = 128
CHUNKS = D // LANES
UNITS = CHUNKS * CPD
SMALL = 6 << 20
AXES = ("row", "col")
VMEM = pl.BlockSpec(memory_space=pltpu.VMEM)


def _flat(x, y, z, core):
    return ((((z // 2) * 4 + x) * 2 + z % 2) * 4 + y) * 2 + core


LINKS = {
    "xa": lambda x, y, z: (x ^ 1, y, z),
    "xb": lambda x, y, z: (3 - x, y, z),
    "xaya": lambda x, y, z: (x ^ 1, y ^ 1, z),
    "xbyb": lambda x, y, z: (3 - x, 3 - y, z),
    "ya": lambda x, y, z: (x, y ^ 1, z),
    "yb": lambda x, y, z: (x, 3 - y, z),
    "za": lambda x, y, z: (x, y, z ^ 1),
    "zb": lambda x, y, z: (x, y, (z - 1) % 8 if z % 2 == 0 else (z + 1) % 8),
}


def swap(block, link0, link1):
    pairs = []
    for x, y, z, core in itertools.product(range(4), range(4), range(8), range(2)):
        pairs.append((_flat(x, y, z, core), _flat(*LINKS[(link0, link1)[core]](x, y, z), core)))
    return lax.ppermute(block, AXES, pairs)


def shift(block, sign):
    pairs = []
    for x, y, z, core in itertools.product(range(4), range(4), range(8), range(2)):
        step = 2 * sign * (1 if (z + core) % 2 == 0 else -1)
        pairs.append((_flat(x, y, z, core), _flat(x, y, (z + step) % 8, core)))
    return lax.ppermute(block, AXES, pairs)


def swap_cores(block):
    return lax.ppermute(block, AXES, [(i, i ^ 1) for i in range(256)])


def units_kernel(emb, out):
    e = emb[...]
    unit = (e / jnp.sqrt(jnp.sum(e * e, axis=1, keepdims=True) + 1e-06)).astype(BF)
    for f in range(CHUNKS):
        out[f * CPD : (f + 1) * CPD, :] = unit[:, f * LANES : (f + 1) * LANES]


def pack_kernel(unit, margin, group, whole):
    row = lax.broadcasted_iota(jnp.int32, (META, LANES), 0)
    meta = jnp.where(row == 0, margin[...], jnp.where(row == 1, group[...], 0)).astype(F32).astype(BF)
    whole[:UNITS, :] = unit[...]
    whole[UNITS:, :] = meta


def pack(embeddings, margin, group):
    params = pltpu.CompilerParams(vmem_limit_bytes=SMALL)
    unit = pl.pallas_call(
        units_kernel,
        out_shape=jax.ShapeDtypeStruct((UNITS, LANES), BF),
        in_specs=[VMEM],
        out_specs=VMEM,
        compiler_params=params,
        name="units",
    )(embeddings)
    return pl.pallas_call(
        pack_kernel,
        out_shape=jax.ShapeDtypeStruct((UNITS + META, LANES), BF),
        in_specs=[VMEM] * 3,
        out_specs=VMEM,
        compiler_params=params,
        name="pack",
    )(unit, margin.reshape(1, CPD), group.reshape(1, CPD))


TB = 8


def units(ref, k):
    at = k * UNITS
    return jnp.concatenate([ref[at + f * CPD : at + (f + 1) * CPD, :] for f in range(CHUNKS)], axis=1)


def marks(ref, k):
    meta = ref[ref.shape[0] - META :, :].astype(F32)
    return meta[2 * k : 2 * k + 1], meta[2 * k + 1 : 2 * k + 2]


def blocks(ref):
    return (ref.shape[0] - META) // UNITS


def pair_kernel(n_r, n_c, n_sum, *refs):
    r_in, c_in, rest = refs[:n_r], refs[n_r : n_r + n_c], refs[n_r + n_c :]
    sums, outs = rest[:n_sum], rest[n_sum:]
    r_blocks, c_blocks = ([(ref, k) for ref in v for k in range(blocks(ref))] for v in (r_in, c_in))
    acc, r_margin, r_group = [], [], []
    for i in range(0, len(r_blocks), 2):
        meta = [marks(ref, k) for ref, k in r_blocks[i : i + 2]]
        r_margin.append(jnp.concatenate([jnp.broadcast_to(m * 0.0005, (CPD, CPD)).T for m, _ in meta], axis=0))
        r_group.append(jnp.concatenate([jnp.broadcast_to(g, (CPD, CPD)).T for _, g in meta], axis=0))
        acc.append(None)
    halves = [(ref, o) for ref in sums for o in range(0, ref.shape[0], 2 * CPD)]
    for i, (ref, o) in enumerate(halves):
        acc[i] = ref[o : o + 2 * CPD, :]
    for t in range(0, len(c_blocks), TB):
        tile = c_blocks[t : t + TB]
        meta = [marks(ref, k) for ref, k in tile]
        ct = jnp.concatenate([units(ref, k) for ref, k in tile], axis=0)
        for i in range(len(acc)):
            rt = jnp.concatenate([units(ref, k) for ref, k in r_blocks[2 * i : 2 * i + 2]], axis=0)
            cos = lax.dot_general(rt, ct, (((1,), (1,)), ((), ())), preferred_element_type=F32)
            parts = []
            for k, (m, g) in enumerate(meta):
                over = jnp.maximum(cos[:, k * LANES : (k + 1) * LANES] - r_margin[i] - m * 0.0005, 0.0)
                parts.append(jnp.where(r_group[i] != g, over, 0.0).astype(BF))
            part = jnp.dot(jnp.concatenate(parts, axis=1), ct, preferred_element_type=F32)
            acc[i] = part if acc[i] is None else acc[i] + part
    halves = [(ref, o) for ref in outs for o in range(0, ref.shape[0], 2 * CPD)]
    for i, (ref, o) in enumerate(halves):
        ref[o : o + acc[i].shape[0], :] = acc[i].astype(ref.dtype)


def pair(r_in, c_in, out_dtype, sums=()):
    rows, cols = (sum(blocks(a) for a in v) * CPD for v in (r_in, c_in))
    return pl.pallas_call(
        functools.partial(pair_kernel, len(r_in), len(c_in), len(sums)),
        out_shape=[jax.ShapeDtypeStruct((blocks(a) * CPD, D), out_dtype) for a in r_in],
        in_specs=[VMEM] * (len(r_in) + len(c_in) + len(sums)),
        out_specs=[VMEM] * len(r_in),
        compiler_params=pltpu.CompilerParams(vmem_limit_bytes=20 << 20),
        cost_estimate=pl.CostEstimate(
            flops=4 * rows * cols * D, bytes_accessed=(cols + rows) * D * 2, transcendentals=0
        ),
        name="pair",
    )(*r_in, *c_in, *sums)


def join_kernel(*refs):
    ins, out = refs[:-1], refs[-1]
    row = lax.broadcasted_iota(jnp.int32, (META, LANES), 0)
    meta = jnp.zeros((META, LANES), F32)
    for i, ref in enumerate(ins):
        out[i * UNITS : (i + 1) * UNITS, :] = ref[:UNITS, :]
        margin, group = marks(ref, 0)
        meta = jnp.where(row == 2 * i, margin, jnp.where(row == 2 * i + 1, group, meta))
    out[len(ins) * UNITS :, :] = meta.astype(BF)


def join(*ins):
    return pl.pallas_call(
        join_kernel,
        out_shape=jax.ShapeDtypeStruct((len(ins) * UNITS + META, LANES), BF),
        in_specs=[VMEM] * len(ins),
        out_specs=VMEM,
        compiler_params=pltpu.CompilerParams(vmem_limit_bytes=SMALL),
        name="join",
    )(*ins)


def final_kernel(rate, emb, own, *refs):
    arrived, out = refs[:-1], refs[-1]
    e = emb[...]
    lengths = jnp.sqrt(jnp.sum(e * e, axis=1, keepdims=True) + 1e-06)
    unit = e / lengths
    grad = 4.0 * sum((ref[...].astype(F32) for ref in arrived), own[...])
    radial = jnp.sum(unit * grad, axis=1, keepdims=True)
    out[...] = e - rate * ((grad - unit * radial) / lengths)


def per_device(embeddings, margin, group):
    classes = embeddings.shape[0] * lax.axis_size("row") * lax.axis_size("col")
    whole = pack(embeddings, margin, group)

    near = swap(whole, "za", "zb")
    square = [swap(whole, a, b) for a, b in (("xaya", "xbyb"), ("xa", "xb"), ("ya", "yb"))]
    both = join(whole, near)
    back = swap(both, "zb", "za")
    c0 = join(*square, whole)
    far, ahead = shift(back, 1), swap(back, "za", "zb")
    c3, c1, c2 = (swap(c0, b, a) for a, b in (("xaya", "xbyb"), ("xa", "xb"), ("ya", "yb")))
    e0 = swap_cores(c0)
    (p_far,) = pair([far], [c0, c1], F32)
    c2, c3, ahead, p_far = lax.optimization_barrier((c2, c3, ahead, p_far))
    e1, e2, e3 = swap_cores(c1), swap_cores(c2), swap_cores(c3)
    cols = [c0, c1, c2, c3, e0, e1, e2, e3]
    (p_far,) = pair([far], [c2, c3, e0, e1], F32, [p_far])
    (p_far,) = pair([far], [e2, e3], BF, [p_far])
    q = swap(p_far, "zb", "za")
    p_ahead, p_back = pair([ahead, back], cols, F32)
    q = swap((p_ahead + q).astype(BF), "za", "zb")
    (p_near,) = pair([near], cols, BF)
    q_near = swap(p_near, "za", "zb")
    (p_own,) = pair([whole], cols, F32)
    p_back = (p_back + q).astype(BF)
    arrived = (q_near, shift(p_back[CPD:], -1), swap(p_back[:CPD], "zb", "za"))

    rate = D * math.sqrt(D) / (3.0 * math.sqrt(classes))
    return pl.pallas_call(
        functools.partial(final_kernel, rate),
        out_shape=jax.ShapeDtypeStruct((CPD, D), F32),
        in_specs=[VMEM] * 5,
        out_specs=VMEM,
        compiler_params=pltpu.CompilerParams(vmem_limit_bytes=SMALL),
        name="final",
    )(embeddings, p_own, *arrived)


def solution(mesh):
    in_specs = (P(("row", "col"), None), P(("row", "col")), P(("row", "col")))
    out_specs = P(("row", "col"), None)
    return jax.shard_map(per_device, mesh=mesh, in_specs=in_specs, out_specs=out_specs, check_vma=False)
```
